512 devices in a mesh: row: 32 (over x, y), span: 16 (over z, core).
Axes of the slice: x: 4, y: 8, z: 8, core: 2. Of those that a mesh axis runs over, the one named last changes fastest.
Arguments:
- velocity: float32 [3, 16, 512, 4096], P(None, 'span', 'row'), may hold values from -6 to 6
- row_counts: int32 [32], replicated, may hold values from 1 to 16, as said below
- y_metric: float32 [257], replicated, may hold values from 0.5 to 2
- y_curvature: float32 [257], replicated, may hold values from -3 to 3
Outputs:
- rhs: float32 [3, 16, 512, 4096], P(None, 'span', 'row')
The draws below stay inside these ranges and needn't reach their ends.
Inputs may be any that keep to these rules, and one draw needn't show every extreme that they name: Index r of row holds row_counts[r] grid rows in its first row_counts[r] slots, following those of index r - 1; the counts sum to 257.
All inputs are finite; a program needn't handle non-finite values.
Results may differ from the reference program's by a relative error of at most 0.000059.
Values sent between devices are 32-bit elements; how exact they have to be, the bound alone decides.
A program may use at most 64 MiB of HBM per device.

```python
import math
import jax
import jax.numpy as jnp
from jax import lax

NX = 4096
ROWS_DEV = 8
CY = 16
NY_LIVE = 257
NY_PAD = 512
NZ = 16
N_ROW = 32


def draw_row_counts(key, part):
    key = jax.random.fold_in(key, 11)
    live_total = ROWS_DEV * N_ROW + 1
    short_run = max(1, ((CY - ROWS_DEV) * N_ROW - 1) // (CY - 1))
    other_count = N_ROW - short_run
    deficit = CY * other_count - (live_total - short_run)
    key_removal, key_shuffle, key_rotate = jax.random.split(key, 3)
    removal_order = jax.random.permutation(key_removal, (other_count - 1) * (CY - 1)).astype(jnp.int32)
    removed = (removal_order < deficit).astype(jnp.int32).reshape(other_count - 1, CY - 1)
    remaining = (CY - jnp.sum(removed, axis=1)).astype(jnp.int32)
    full_first = jnp.concatenate([jnp.full((1,), CY, dtype=jnp.int32), remaining])
    shuffle_order = jax.random.permutation(key_shuffle, other_count).astype(jnp.int32)
    shuffled = jnp.take(full_first, shuffle_order)
    sequence = jnp.concatenate([jnp.ones((short_run,), dtype=jnp.int32), shuffled])
    rotation = jax.random.randint(key_rotate, (), 0, N_ROW, dtype=jnp.int32)
    positions = (jnp.arange(N_ROW, dtype=jnp.int32) - rotation) % N_ROW
    return jnp.take(sequence, positions).astype(jnp.int32)


def levels(rng, dims, pieces, smallest, largest):
    def one(axis_at, blocks):
        steps = jax.random.uniform(jax.random.fold_in(jax.random.fold_in(rng, 6), axis_at), (blocks,), jnp.float32, smallest / len(pieces), largest / len(pieces))
        return jnp.repeat(jnp.exp(steps), dims[axis_at] // blocks).reshape((-1,) + (1,) * (len(dims) - axis_at - 1))

    level = one(*pieces[0])
    for cut in pieces[1:]:
        level = level * one(*cut)
    return level


def scatter_about(own_key, dims, width, most, pieces=(), held_as=jnp.bfloat16):
    gain = levels(own_key, dims, pieces, -0.22, 0.18) if pieces else 1.0
    values = jax.random.normal(own_key, dims, jnp.float32) * width * gain
    return jnp.minimum(jnp.maximum(values, -most), most).astype(held_as)


def setup_inputs(seed: int = 0) -> dict:
    key_list = jax.random.split(jax.random.key(seed), 5)
    velocity = scatter_about(key_list[0], (3, NZ, NY_PAD, NX), 1.0, 6.0, ((1, 16), (2, 32)), jnp.float32)
    row_counts = draw_row_counts(jax.random.fold_in(key_list[4], 71), 0)
    y_metric = jnp.clip(jnp.exp(jax.random.uniform(key_list[2], (NY_LIVE,), jnp.float32, math.log(0.5), math.log(2.0))), 0.5, 2.0)
    y_curvature = scatter_about(key_list[3], (NY_LIVE,), 0.5, 3.0, (), jnp.float32)
    return dict(velocity=velocity, row_counts=row_counts, y_metric=y_metric, y_curvature=y_curvature)


first_alpha = 1.0 / 3.0
first_near = 14.0 / 9.0
first_far = 1.0 / 9.0
second_alpha = 2.0 / 11.0
second_near = 12.0 / 11.0
second_far = 3.0 / 11.0
viscosity = 0.2


def wavenumbers(angles):
    first_symbol = (first_near * jnp.sin(angles) + 0.5 * first_far * jnp.sin(2.0 * angles)) / (1.0 + 2.0 * first_alpha * jnp.cos(angles))
    second_symbol = (2.0 * second_near * (1.0 - jnp.cos(angles)) + 0.5 * second_far * (1.0 - jnp.cos(2.0 * angles))) / (1.0 + 2.0 * second_alpha * jnp.cos(angles))
    return first_symbol, second_symbol


def span_tables(plane_count):
    positions = jnp.arange(plane_count, dtype=jnp.int32)
    angles = (2.0 * math.pi / plane_count) * positions.astype(jnp.float32)
    first_symbol, second_symbol = wavenumbers(angles)
    winding = ((positions[:, None] - positions[None, :])[:, :, None] * positions[None, None, :]) % plane_count
    phases = (2.0 * math.pi / plane_count) * winding.astype(jnp.float32)
    span_first = -jnp.sum(first_symbol * jnp.sin(phases), axis=2) / plane_count
    span_second = -jnp.sum(second_symbol * jnp.cos(phases), axis=2) / plane_count
    return span_first, span_second


def row_maps(row_counts, slots, live_total):
    ranks = row_counts.shape[0]
    starts = jnp.cumsum(row_counts) - row_counts
    within = jnp.arange(slots, dtype=jnp.int32)
    alive = within[None, :] < row_counts[:, None]
    source = jnp.where(alive, starts[:, None] + within[None, :], live_total).reshape(-1).astype(jnp.int32)
    grid_rows = jnp.arange(live_total, dtype=jnp.int32)
    owner = jnp.sum((starts[None, :] <= grid_rows[:, None]).astype(jnp.int32), axis=1) - 1
    picked = jnp.arange(ranks, dtype=jnp.int32)[None, :] == owner[:, None]
    owner_start = jnp.sum(jnp.where(picked, starts[None, :], 0), axis=1)
    target = (owner * slots + grid_rows - owner_start).astype(jnp.int32)
    return alive.reshape(-1), source, target


def restore(values, source, axis):
    zero_slab = jnp.zeros_like(lax.slice_in_dim(values, 0, 1, axis=axis))
    return jnp.take(jnp.concatenate([values, zero_slab], axis=axis), source, axis=axis)


def spectral_pair(field, axis):
    length = field.shape[axis]
    angles = (2.0 * math.pi / length) * jnp.arange(length, dtype=jnp.int32).astype(jnp.float32)
    first_symbol, second_symbol = wavenumbers(angles)
    shape = [1] * field.ndim
    shape[axis] = length
    coeffs = jnp.fft.fft(field, axis=axis)
    first_part = jnp.real(jnp.fft.ifft(coeffs * (1j * first_symbol.reshape(shape)), axis=axis))
    second_part = jnp.real(jnp.fft.ifft(coeffs * (-second_symbol.reshape(shape)), axis=axis))
    return first_part.astype(field.dtype), second_part.astype(field.dtype)


def reference(velocity, row_counts, y_metric, y_curvature):
    alive, source, target = row_maps(row_counts, CY, NY_LIVE)
    alive_rows = alive.astype(jnp.float32)[:, None]
    span_first, span_second = span_tables(NZ)
    metric = y_metric[:, None]
    curvature = y_curvature[:, None]

    def plane_rhs(plane_index):
        layer = lax.dynamic_index_in_dim(velocity, plane_index, 1, keepdims=False)
        first_x, second_x = spectral_pair(layer, 2)
        first_eta, second_eta = spectral_pair(jnp.take(layer, target, axis=1), 1)
        first_y = restore(metric * first_eta, source, 1)
        second_y = restore(metric * metric * second_eta + curvature * first_eta, source, 1)
        row_first = lax.dynamic_index_in_dim(span_first, plane_index, 0, keepdims=False)
        row_second = lax.dynamic_index_in_dim(span_second, plane_index, 0, keepdims=False)
        first_z = jnp.einsum("n,cnyx->cyx", row_first, velocity, precision=lax.Precision.HIGHEST)
        second_z = jnp.einsum("n,cnyx->cyx", row_second, velocity, precision=lax.Precision.HIGHEST)
        convect = layer[0] * first_x + layer[1] * first_y + layer[2] * first_z
        total = -convect + viscosity * (second_x + second_y + second_z)
        return total * alive_rows

    stacked = lax.map(plane_rhs, jnp.arange(NZ, dtype=jnp.int32))
    return jnp.transpose(stacked, (1, 0, 2, 3))
```

```python
import functools
import math

import jax
import jax.numpy as jnp
import ml_dtypes
import numpy as np
from jax import lax
from jax.experimental import pallas as pl
from jax.experimental.pallas import tpu as pltpu
from jax.sharding import PartitionSpec as P

MESH = pl.DeviceIdType.MESH
viscosity = 0.2
LANES = 128
STATES = 8


def scheme(alpha, first):
    root = math.sqrt(1.0 - 4.0 * alpha * alpha)
    decay = (1.0 - root) / (2.0 * alpha)

    def res(s):
        return (-decay) ** abs(s) / root

    def tap(s):
        if first:
            return 0.5 * 14.0 / 9.0 * (res(s - 1) - res(s + 1)) + 0.25 / 9.0 * (res(s - 2) - res(s + 2))
        return (
            12.0 / 11.0 * (res(s - 1) - 2.0 * res(s) + res(s + 1))
            + 0.25 * 3.0 / 11.0 * (res(s - 2) - 2.0 * res(s) + res(s + 2))
        )

    amp = tap(2) / decay**2
    return dict(tap=tap, log=math.log(decay), amp=amp, near=tap(1) + amp * decay, centre=tap(0))


FIRST = scheme(1.0 / 3.0, True)
SECOND = scheme(2.0 / 11.0, False)


def split_table(table):
    high = table.astype(ml_dtypes.bfloat16)
    return jnp.asarray(high), jnp.asarray((table - high.astype(np.float64)).astype(ml_dtypes.bfloat16))


def line_table():
    table = np.zeros((2 * LANES, 2 * LANES))
    for p in range(2 * LANES):
        for q in range(LANES):
            shift = p - LANES // 2 - q
            table[p, q] = FIRST["tap"](shift)
            table[p, LANES + q] = viscosity * SECOND["tap"](shift)
    return table


def plane_table(count):
    table = np.zeros((2, count, 8, count, 8))
    for m in range(count):
        for n in range(count):
            for turn in range(-40, 41):
                shift = n - m + turn * count
                for row in range(8):
                    table[0, m, row, n, row] += FIRST["tap"](shift)
                    table[1, m, row, n, row] += viscosity * SECOND["tap"](shift)
    return table.reshape(16 * count, 8 * count)


def split(values):
    high = values.astype(jnp.bfloat16)
    return high, (values - high.astype(jnp.float32)).astype(jnp.bfloat16)


def product(left, right):
    dot = functools.partial(jnp.dot, preferred_element_type=jnp.float32)
    return dot(left[0], right[0]) + (dot(left[0], right[1]) + dot(left[1], right[0]))


def power(log, steps):
    size = jnp.exp(steps.astype(jnp.float32) * log)
    return jnp.where(steps % 2 == 0, size, -size)


def iota(shape, axis):
    return lax.broadcasted_iota(jnp.int32, shape, axis)


def partner(index, me, count):
    half = count // 2
    step = jnp.where(index % 2 == 1, half - (index + 1) // 2, half + index // 2)
    return (me + step) % count


def kernel(
    ranks, planes, live_total, length,
    v, counts, metric, curvature, line_high, line_low, plane_high, plane_low,
    out,
    pad_high, pad_low, z_in, z_out, z_back, s_out, s_in, s_mid, s_back, s_weight, y_weight,
    z_send, z_recv, zb_send, zb_recv, s_send, s_recv, sb_send, sb_recv,
):
    my_row, my_plane = lax.axis_index("row"), lax.axis_index("span")
    z_cols, s_cols = length // planes, length // ranks
    pieces = [(half, part) for half in range(2) for part in range(z_cols // LANES)]

    def lanes(start, size=LANES):
        return pl.ds(pl.multiple_of(start, LANES), size)

    def forth(piece, source, target):
        half, part = pieces[piece]
        return pltpu.make_async_remote_copy(
            src_ref=v.at[:, half, :, lanes(target * z_cols + part * LANES)],
            dst_ref=z_in.at[piece, source],
            send_sem=z_send.at[piece, target],
            recv_sem=z_recv.at[piece, source],
            device_id={"span": target},
            device_id_type=MESH,
        )

    def back(piece, source, target):
        half, part = pieces[piece]
        return pltpu.make_async_remote_copy(
            src_ref=z_out.at[piece, target],
            dst_ref=z_back.at[:, half, :, lanes(source * z_cols + part * LANES)],
            send_sem=zb_send.at[piece, target],
            recv_sem=zb_recv.at[piece, source],
            device_id={"span": target},
            device_id_type=MESH,
        )

    def state_forth(source, target):
        return pltpu.make_async_remote_copy(
            src_ref=s_out.at[:, :, lanes(target * s_cols, s_cols)],
            dst_ref=s_in.at[source],
            send_sem=s_send.at[target],
            recv_sem=s_recv.at[source],
            device_id={"row": target},
            device_id_type=MESH,
        )

    def state_back(source, target):
        return pltpu.make_async_remote_copy(
            src_ref=s_mid.at[target],
            dst_ref=s_back.at[:, :, lanes(source * s_cols, s_cols)],
            send_sem=sb_send.at[target],
            recv_sem=sb_recv.at[source],
            device_id={"row": target},
            device_id_type=MESH,
        )

    def over_planes(act):
        pl.loop(0, planes - 1)(lambda index: act(partner(index, my_plane, planes)))

    def over_ranks(act):
        pl.loop(0, ranks - 1)(lambda index: act(partner(index, my_row, ranks)))

    barrier = pltpu.get_barrier_semaphore()
    over_planes(lambda p: pl.semaphore_signal(barrier, 1, device_id={"span": p}, device_id_type=MESH))
    over_ranks(lambda p: pl.semaphore_signal(barrier, 1, device_id={"row": p}, device_id_type=MESH))

    count = counts[my_row]
    start = jnp.int32(0)
    for rank in range(ranks):
        start = start + jnp.where(rank < my_row, counts[rank], 0)

    kind = iota((STATES, LANES), 0)
    decay_log = jnp.where(kind % 2 == 0, FIRST["log"], SECOND["log"])
    for k in range(16):
        steps = jnp.where(kind < 2, jnp.maximum(count - 1 - k, 0), k)
        weight = jnp.where(kind < 4, power(decay_log, steps), 0.0)
        weight = jnp.where((kind == 4) & (k == 0), 1.0, weight)
        weight = jnp.where((kind == 5) & (count - 1 == k), 1.0, weight)
        s_weight[k] = jnp.where(k < count, weight, 0.0)

    pl.semaphore_wait(barrier, planes + ranks - 2)

    for piece in range(len(pieces)):
        over_planes(lambda p, piece=piece: forth(piece, my_plane, p).start())

    @pl.loop(0, length // LANES)
    def _(tile):
        at = lanes(tile * LANES)
        for c in range(3):
            total = jnp.zeros((STATES, LANES), jnp.float32)
            for k in range(16):
                total = total + s_weight[k] * v[c, k // 8, pl.ds(k % 8, 1), at]
            s_out[c, :, at] = total

    over_ranks(lambda p: state_forth(my_row, p).start())
    s_in[my_row] = s_out[:, :, lanes(my_row * s_cols, s_cols)]
    for piece, (half, part) in enumerate(pieces):
        z_in[piece, my_plane] = v[:, half, :, lanes(my_plane * z_cols + part * LANES)]

    for c in range(3):
        turned = pltpu.roll(v[c].reshape(16, length), LANES // 2, 1)
        high, low = split(turned)
        rows = pl.ds(16 * c, 16)
        pad_high[rows, pl.ds(0, length)] = high
        pad_low[rows, pl.ds(0, length)] = low
        pad_high[rows, pl.ds(length, LANES)] = high[:, :LANES]
        pad_low[rows, pl.ds(length, LANES)] = low[:, :LANES]

    group = 4

    def along_x(step):
        def windows(ref):
            return jnp.concatenate(
                [ref[:, lanes((step * group + i) * LANES, 2 * LANES)] for i in range(group)], axis=0
            )

        both = product((windows(pad_high), windows(pad_low)), (line_high[...], line_low[...]))
        for i in range(group):
            at = lanes((step * group + i) * LANES)
            wind = v[0, :, :, at].reshape(16, LANES)
            for c in range(3):
                rows = slice(48 * i + 16 * c, 48 * i + 16 * c + 16)
                part = both[rows, LANES:] - wind * both[rows, :LANES]
                out[c, :, :, at] = part.reshape(2, 8, LANES)

    steps_x = length // (LANES * group)
    pl.loop(0, steps_x // 2)(along_x)

    def along_z(piece):
        over_planes(lambda p: forth(piece, p, my_plane).wait_recv())
        held = [z_in[piece, :, c].reshape(8 * planes, LANES) for c in range(3)]
        both = product((plane_high[...], plane_low[...]), split(jnp.concatenate(held, axis=1)))
        for c in range(3):
            at = slice(c * LANES, (c + 1) * LANES)
            part = both[8 * planes :, at] - held[2] * both[: 8 * planes, at]
            z_out[piece, :, c] = part.reshape(planes, 8, LANES)
        over_planes(lambda p: back(piece, my_plane, p).start())
        half, part = pieces[piece]
        z_back[:, half, :, lanes(my_plane * z_cols + part * LANES)] = z_out[piece, my_plane]

    def over_y():
        size = ranks * STATES
        row_rank, row_kind = iota((size, size), 0) // STATES, iota((size, size), 0) % STATES
        col_rank, col_kind = iota((size, size), 1) // STATES, iota((size, size), 1) % STATES
        row_start = row_count = col_start = col_count = jnp.zeros((size, size), jnp.int32)
        for rank in range(ranks):
            held = counts[rank]
            row_start = row_start + jnp.where(rank < row_rank, held, 0)
            col_start = col_start + jnp.where(rank < col_rank, held, 0)
            row_count = jnp.where(rank == row_rank, held, row_count)
            col_count = jnp.where(rank == col_rank, held, col_count)
        ahead = row_start - col_start - col_count
        ahead = jnp.where(ahead < 0, ahead + live_total, ahead)
        behind = col_start - row_start - row_count
        behind = jnp.where(behind < 0, behind + live_total, behind)
        log = jnp.where(row_kind % 2 == 0, FIRST["log"], SECOND["log"])
        same = power(log, jnp.where(row_kind < 2, ahead, behind))
        matrix = jnp.where((row_kind == col_kind) & (row_kind < 4), same, 0.0)
        matrix = jnp.where((row_kind == 4) & (col_kind == 5) & (ahead == 0), 1.0, matrix)
        matrix = jnp.where((row_kind == 5) & (col_kind == 4) & (behind == 0), 1.0, matrix)
        matrix = split(matrix)
        over_ranks(lambda p: state_forth(p, my_row).wait_recv())
        held = [s_in[:, c].reshape(size, s_cols) for c in range(3)]
        both = product(matrix, split(jnp.concatenate(held, axis=1)))
        for c in range(3):
            s_mid[:, c] = both[:, c * s_cols : (c + 1) * s_cols].reshape(ranks, STATES, s_cols)
        over_ranks(lambda p: state_back(my_row, p).start())
        s_back[:, :, lanes(my_row * s_cols, s_cols)] = s_mid[my_row]

    along_z(0)
    pl.loop(steps_x // 2, steps_x)(along_x)
    along_z(1)
    over_y()
    for piece in range(2, len(pieces)):
        along_z(piece)

    for half in range(2):
        slot = iota((8, LANES), 0) + 8 * half
        stretch = jnp.zeros((8, LANES), jnp.float32)
        bend = jnp.zeros((8, LANES), jnp.float32)
        for k in range(8 * half, 8 * half + 8):
            grid_row = jnp.minimum(start + k, live_total - 1)
            stretch = jnp.where(slot == k, metric[grid_row], stretch)
            bend = jnp.where(slot == k, curvature[grid_row], bend)
        live = slot < count
        tail = jnp.maximum(count - slot, 0)
        for term in range(16 + 6):
            if term < 16:
                away = jnp.abs(term - slot)
                one = FIRST["amp"] * power(FIRST["log"], away) + jnp.where(away == 1, FIRST["near"], 0.0)
                one = jnp.where(away == 0, 0.0, jnp.where(term > slot, one, -one))
                two = SECOND["amp"] * power(SECOND["log"], away) + jnp.where(away == 1, SECOND["near"], 0.0)
                two = jnp.where(away == 0, SECOND["centre"], two)
                used = live & (term < count)
            else:
                one = two = jnp.zeros((8, LANES), jnp.float32)
                used = live
                if term == 16:
                    one = -FIRST["amp"] * power(FIRST["log"], slot + 1)
                if term == 17:
                    two = SECOND["amp"] * power(SECOND["log"], slot + 1)
                if term == 18:
                    one = FIRST["amp"] * power(FIRST["log"], tail)
                if term == 19:
                    two = SECOND["amp"] * power(SECOND["log"], tail)
                if term == 20:
                    one = jnp.where(slot == 0, -FIRST["near"], 0.0)
                    two = jnp.where(slot == 0, SECOND["near"], 0.0)
                if term == 21:
                    one = jnp.where(tail == 1, FIRST["near"], 0.0)
                    two = jnp.where(tail == 1, SECOND["near"], 0.0)
            y_weight[term, half, 0] = jnp.where(used, stretch * one, 0.0)
            y_weight[term, half, 1] = jnp.where(
                used, viscosity * (stretch * stretch * two + bend * one), 0.0
            )

    over_ranks(lambda p: state_back(p, my_row).wait_recv())

    @pl.loop(0, length // LANES)
    def _(tile):
        at = lanes(tile * LANES)
        sums = [[[jnp.zeros((8, LANES), jnp.float32)] * 2 for _ in range(2)] for _ in range(3)]
        for term in range(16 + 6):
            for c in range(3):
                if term < 16:
                    line = v[c, term // 8, pl.ds(term % 8, 1), at]
                else:
                    line = s_back[c, pl.ds(term - 16, 1), at]
                for half in range(2):
                    sums[c][half] = [sums[c][half][i] + y_weight[term, half, i] * line for i in range(2)]
        for half in range(2):
            wind = v[1, half, :, at]
            for c in range(3):
                out[c, half, :, at] += sums[c][half][1] - wind * sums[c][half][0]

    per_half = len(pieces) // 2
    for half in range(2):
        for piece in range(half * per_half, (half + 1) * per_half):
            over_planes(lambda p, piece=piece: back(piece, p, my_plane).wait_recv())
        live = iota((8, LANES), 0) + 8 * half < count

        @pl.loop(0, length // LANES)
        def _(tile, half=half, live=live):
            at = lanes(tile * LANES)
            for c in range(3):
                out[c, half, :, at] = jnp.where(live, out[c, half, :, at] + z_back[c, half, :, at], 0.0)

    for piece in range(len(pieces)):
        over_planes(lambda p, piece=piece: forth(piece, my_plane, p).wait_send())
        over_planes(lambda p, piece=piece: back(piece, my_plane, p).wait_send())
    over_ranks(lambda p: state_forth(my_row, p).wait_send())
    over_ranks(lambda p: state_back(my_row, p).wait_send())


def local(ranks, planes, velocity, row_counts, y_metric, y_curvature):
    length = velocity.shape[3]
    live_total = y_metric.shape[0]
    z_cols, s_cols = length // planes, length // ranks
    pieces = 2 * z_cols // LANES
    vmem = pl.BlockSpec(memory_space=pltpu.VMEM)
    smem = pl.BlockSpec(memory_space=pltpu.SMEM)
    whole = (3, 2, 8, length)
    dma = pltpu.SemaphoreType.DMA
    f32 = jnp.float32
    result = pl.pallas_call(
        functools.partial(kernel, ranks, planes, live_total, length),
        out_shape=jax.ShapeDtypeStruct(whole, f32),
        in_specs=[vmem, smem, smem, smem, vmem, vmem, vmem, vmem],
        out_specs=vmem,
        scratch_shapes=[
            pltpu.VMEM((48, length + LANES), jnp.bfloat16),
            pltpu.VMEM((48, length + LANES), jnp.bfloat16),
            pltpu.VMEM((pieces, planes, 3, 8, LANES), f32),
            pltpu.VMEM((pieces, planes, 3, 8, LANES), f32),
            pltpu.VMEM(whole, f32),
            pltpu.VMEM((3, STATES, length), f32),
            pltpu.VMEM((ranks, 3, STATES, s_cols), f32),
            pltpu.VMEM((ranks, 3, STATES, s_cols), f32),
            pltpu.VMEM((3, STATES, length), f32),
            pltpu.VMEM((16, STATES, LANES), f32),
            pltpu.VMEM((22, 2, 2, 8, LANES), f32),
            dma((pieces, planes)),
            dma((pieces, planes)),
            dma((pieces, planes)),
            dma((pieces, planes)),
            dma((ranks,)),
            dma((ranks,)),
            dma((ranks,)),
            dma((ranks,)),
        ],
        compiler_params=pltpu.CompilerParams(
            collective_id=0, has_side_effects=True, vmem_limit_bytes=32 * 1024 * 1024
        ),
        cost_estimate=pl.CostEstimate(flops=10**9, bytes_accessed=2 * 10**6, transcendentals=10**5),
    )(
        velocity.reshape(whole), row_counts, y_metric, y_curvature,
        *split_table(line_table()), *split_table(plane_table(planes)),
    )
    return result.reshape(velocity.shape)


def solution(mesh):
    return jax.shard_map(
        functools.partial(local, mesh.shape["row"], mesh.shape["span"]),
        mesh=mesh,
        in_specs=(P(None, "span", "row", None), P(), P(), P()),
        out_specs=P(None, "span", "row", None),
        check_vma=False,
    )
```

```python
import functools
import math

import jax
import jax.numpy as jnp
import numpy as np
from jax import lax
from jax.experimental import pallas as pl
from jax.experimental.pallas import tpu as pltpu
from jax.sharding import PartitionSpec as P

MESH = pl.DeviceIdType.MESH
viscosity = 0.2
LANES = 128
STATES = 8


def scheme(alpha, first):
    root = math.sqrt(1.0 - 4.0 * alpha * alpha)
    decay = (1.0 - root) / (2.0 * alpha)

    def res(s):
        return (-decay) ** abs(s) / root

    def tap(s):
        if first:
            return 0.5 * 14.0 / 9.0 * (res(s - 1) - res(s + 1)) + 0.25 / 9.0 * (res(s - 2) - res(s + 2))
        return (
            12.0 / 11.0 * (res(s - 1) - 2.0 * res(s) + res(s + 1))
            + 0.25 * 3.0 / 11.0 * (res(s - 2) - 2.0 * res(s) + res(s + 2))
        )

    amp = tap(2) / decay**2
    return dict(tap=tap, log=math.log(decay), amp=amp, near=tap(1) + amp * decay, centre=tap(0))


FIRST = scheme(1.0 / 3.0, True)
SECOND = scheme(2.0 / 11.0, False)


def line_table():
    table = np.zeros((2 * LANES, 2 * LANES))
    for p in range(2 * LANES):
        for q in range(LANES):
            shift = p - LANES // 2 - q
            table[p, q] = FIRST["tap"](shift)
            table[p, LANES + q] = viscosity * SECOND["tap"](shift)
    return table


def plane_table(count):
    table = np.zeros((2, count, 8, count, 8))
    for m in range(count):
        for n in range(count):
            for turn in range(-40, 41):
                shift = n - m + turn * count
                for row in range(8):
                    table[0, m, row, n, row] += FIRST["tap"](shift)
                    table[1, m, row, n, row] += viscosity * SECOND["tap"](shift)
    return table.reshape(16 * count, 8 * count)


def split(values):
    high = values.astype(jnp.bfloat16)
    return high, (values - high.astype(jnp.float32)).astype(jnp.bfloat16)


def product(left, right):
    dot = functools.partial(jnp.dot, preferred_element_type=jnp.float32)
    return dot(left[0], right[0]) + (dot(left[0], right[1]) + dot(left[1], right[0]))


def power(log, steps):
    size = jnp.exp(steps.astype(jnp.float32) * log)
    return jnp.where(steps % 2 == 0, size, -size)


def iota(shape, axis):
    return lax.broadcasted_iota(jnp.int32, shape, axis)


def partner(index, me, count):
    half = count // 2
    step = jnp.where(index % 2 == 1, half - (index + 1) // 2, half + index // 2)
    return (me + step) % count


def kernel(
    ranks, planes, live_total, length,
    v_far, counts_far, metric_far, curvature_far, line_far, plane_far,
    out_far,
    out, v, counts, metric, curvature, line, plane, line_high, line_low, plane_high, plane_low, matrix,
    pad_high, pad_low, z_in, z_out, z_back, s_out, s_in, s_mid, s_back, s_weight, y_weight,
    local_sem, z_send, z_recv, zb_send, zb_recv, s_send, s_recv, sb_send, sb_recv,
):
    my_row, my_plane = lax.axis_index("row"), lax.axis_index("span")
    z_cols, s_cols = length // planes, length // ranks

    def lanes(start, size=LANES):
        return pl.ds(pl.multiple_of(start, LANES), size)

    def forth(half, source, target):
        return pltpu.make_async_remote_copy(
            src_ref=v_far.at[:, half, :, lanes(target * z_cols, z_cols)],
            dst_ref=z_in.at[half, source],
            send_sem=z_send.at[half, target],
            recv_sem=z_recv.at[half, source],
            device_id={"span": target},
            device_id_type=MESH,
        )

    def back(half, source, target):
        return pltpu.make_async_remote_copy(
            src_ref=z_out.at[half, target],
            dst_ref=z_back.at[:, half, :, lanes(source * z_cols, z_cols)],
            send_sem=zb_send.at[half, target],
            recv_sem=zb_recv.at[half, source],
            device_id={"span": target},
            device_id_type=MESH,
        )

    def state_forth(source, target):
        return pltpu.make_async_remote_copy(
            src_ref=s_out.at[:, :, lanes(target * s_cols, s_cols)],
            dst_ref=s_in.at[source],
            send_sem=s_send.at[target],
            recv_sem=s_recv.at[source],
            device_id={"row": target},
            device_id_type=MESH,
        )

    def state_back(source, target):
        return pltpu.make_async_remote_copy(
            src_ref=s_mid.at[target],
            dst_ref=s_back.at[:, :, lanes(source * s_cols, s_cols)],
            send_sem=sb_send.at[target],
            recv_sem=sb_recv.at[source],
            device_id={"row": target},
            device_id_type=MESH,
        )

    def over_planes(act):
        pl.loop(0, planes - 1)(lambda index: act(partner(index, my_plane, planes)))

    def over_ranks(act):
        pl.loop(0, ranks - 1)(lambda index: act(partner(index, my_row, ranks)))

    barrier = pltpu.get_barrier_semaphore()
    over_planes(lambda p: pl.semaphore_signal(barrier, 1, device_id={"span": p}, device_id_type=MESH))
    over_ranks(lambda p: pl.semaphore_signal(barrier, 1, device_id={"row": p}, device_id_type=MESH))
    pairs = [(counts_far, counts), (v_far, v), (metric_far, metric), (curvature_far, curvature)]
    pairs += [(line_far, line), (plane_far, plane)]
    copies = [pltpu.make_async_copy(*pair, local_sem.at[i]) for i, pair in enumerate(pairs)]
    for copy in copies:
        copy.start()

    copies[0].wait()
    count = counts[my_row]
    kind = iota((STATES, LANES), 0)
    decay_log = jnp.where(kind % 2 == 0, FIRST["log"], SECOND["log"])
    for k in range(16):
        steps = jnp.where(kind < 2, jnp.maximum(count - 1 - k, 0), k)
        weight = jnp.where(kind < 4, power(decay_log, steps), 0.0)
        weight = jnp.where((kind == 4) & (k == 0), 1.0, weight)
        weight = jnp.where((kind == 5) & (count - 1 == k), 1.0, weight)
        s_weight[k] = jnp.where(k < count, weight, 0.0)

    pl.semaphore_wait(barrier, planes + ranks - 2)
    over_planes(lambda p: forth(0, my_plane, p).start())
    copies[1].wait()

    @pl.loop(0, length // LANES)
    def _(tile):
        at = lanes(tile * LANES)
        totals = [jnp.zeros((STATES, LANES), jnp.float32)] * 3
        for k in range(16):
            weight = s_weight[k]
            totals = [totals[c] + weight * v[c, k // 8, pl.ds(k % 8, 1), at] for c in range(3)]
        for c in range(3):
            s_out[c, :, at] = totals[c]

    over_ranks(lambda p: state_forth(my_row, p).start())
    over_planes(lambda p: forth(1, my_plane, p).start())
    s_in[my_row] = s_out[:, :, lanes(my_row * s_cols, s_cols)]
    for half in range(2):
        z_in[half, my_plane] = v[:, half, :, lanes(my_plane * z_cols, z_cols)]

    for copy in copies[2:]:
        copy.wait()
    line_high[...], line_low[...] = split(line[...])
    plane_high[...], plane_low[...] = split(plane[...])

    for c in range(3):
        turned = pltpu.roll(v[c].reshape(16, length), LANES // 2, 1)
        high, low = split(turned)
        rows = pl.ds(16 * c, 16)
        pad_high[rows, pl.ds(0, length)] = high
        pad_low[rows, pl.ds(0, length)] = low
        pad_high[rows, pl.ds(length, LANES)] = high[:, :LANES]
        pad_low[rows, pl.ds(length, LANES)] = low[:, :LANES]

    group = 4

    @pl.loop(0, length // (LANES * group))
    def _(step):
        def windows(ref):
            return jnp.concatenate(
                [ref[:, lanes((step * group + i) * LANES, 2 * LANES)] for i in range(group)], axis=0
            )

        both = product((windows(pad_high), windows(pad_low)), (line_high[...], line_low[...]))
        for i in range(group):
            at = lanes((step * group + i) * LANES)
            wind = v[0, :, :, at].reshape(16, LANES)
            for c in range(3):
                rows = slice(48 * i + 16 * c, 48 * i + 16 * c + 16)
                part = both[rows, LANES:] - wind * both[rows, :LANES]
                out[c, :, :, at] = part.reshape(2, 8, LANES)

    def along_z(half):
        over_planes(lambda p: forth(half, p, my_plane).wait_recv())
        for part in range(z_cols // LANES):
            cut = slice(part * LANES, (part + 1) * LANES)
            held = [z_in[half, :, c, :, cut].reshape(8 * planes, LANES) for c in range(3)]
            both = product((plane_high[...], plane_low[...]), split(jnp.concatenate(held, axis=1)))
            for c in range(3):
                at = slice(c * LANES, (c + 1) * LANES)
                term = both[8 * planes :, at] - held[2] * both[: 8 * planes, at]
                z_out[half, :, c, :, cut] = term.reshape(planes, 8, LANES)
        over_planes(lambda p: back(half, my_plane, p).start())
        z_back[:, half, :, lanes(my_plane * z_cols, z_cols)] = z_out[half, my_plane]

    size = ranks * STATES
    col_rank, col_kind = iota((8, size), 1) // STATES, iota((8, size), 1) % STATES
    row_kind = iota((8, size), 0)
    row_log = jnp.where(row_kind % 2 == 0, FIRST["log"], SECOND["log"])
    col_start = col_count = jnp.zeros((8, size), jnp.int32)
    start = jnp.int32(0)
    for rank in range(ranks):
        col_start = col_start + jnp.where(rank < col_rank, counts[rank], 0)
        col_count = jnp.where(rank == col_rank, counts[rank], col_count)
        start = start + jnp.where(rank < my_row, counts[rank], 0)

    def rank_rows(rank, row_start):
        row_count = counts[rank]
        ahead = row_start - col_start - col_count
        ahead = jnp.where(ahead < 0, ahead + live_total, ahead)
        behind = col_start - row_start - row_count
        behind = jnp.where(behind < 0, behind + live_total, behind)
        same = power(row_log, jnp.where(row_kind < 2, ahead, behind))
        rows = jnp.where((row_kind == col_kind) & (row_kind < 4), same, 0.0)
        rows = jnp.where((row_kind == 4) & (col_kind == 5) & (ahead == 0), 1.0, rows)
        rows = jnp.where((row_kind == 5) & (col_kind == 4) & (behind == 0), 1.0, rows)
        matrix[pl.ds(pl.multiple_of(rank * STATES, STATES), STATES), :] = rows
        return row_start + row_count

    lax.fori_loop(0, ranks, rank_rows, jnp.int32(0))

    def over_y():
        over_ranks(lambda p: state_forth(p, my_row).wait_recv())
        held = [s_in[:, c].reshape(size, s_cols) for c in range(3)]
        both = product(split(matrix[...]), split(jnp.concatenate(held, axis=1)))
        for c in range(3):
            s_mid[:, c] = both[:, c * s_cols : (c + 1) * s_cols].reshape(ranks, STATES, s_cols)
        over_ranks(lambda p: state_back(my_row, p).start())
        s_back[:, :, lanes(my_row * s_cols, s_cols)] = s_mid[my_row]

    along_z(0)
    over_y()

    for half in range(2):
        slot = iota((8, LANES), 0) + 8 * half
        stretch = jnp.zeros((8, LANES), jnp.float32)
        bend = jnp.zeros((8, LANES), jnp.float32)
        for k in range(8 * half, 8 * half + 8):
            grid_row = jnp.minimum(start + k, live_total - 1)
            stretch = jnp.where(slot == k, metric[grid_row], stretch)
            bend = jnp.where(slot == k, curvature[grid_row], bend)
        live = slot < count
        tail = jnp.maximum(count - slot, 0)
        for term in range(16 + 6):
            if term < 16:
                away = jnp.abs(term - slot)
                one = FIRST["amp"] * power(FIRST["log"], away) + jnp.where(away == 1, FIRST["near"], 0.0)
                one = jnp.where(away == 0, 0.0, jnp.where(term > slot, one, -one))
                two = SECOND["amp"] * power(SECOND["log"], away) + jnp.where(away == 1, SECOND["near"], 0.0)
                two = jnp.where(away == 0, SECOND["centre"], two)
                used = live & (term < count)
            else:
                one = two = jnp.zeros((8, LANES), jnp.float32)
                used = live
                if term == 16:
                    one = -FIRST["amp"] * power(FIRST["log"], slot + 1)
                if term == 17:
                    two = SECOND["amp"] * power(SECOND["log"], slot + 1)
                if term == 18:
                    one = FIRST["amp"] * power(FIRST["log"], tail)
                if term == 19:
                    two = SECOND["amp"] * power(SECOND["log"], tail)
                if term == 20:
                    one = jnp.where(slot == 0, -FIRST["near"], 0.0)
                    two = jnp.where(slot == 0, SECOND["near"], 0.0)
                if term == 21:
                    one = jnp.where(tail == 1, FIRST["near"], 0.0)
                    two = jnp.where(tail == 1, SECOND["near"], 0.0)
            y_weight[term, half, 0] = jnp.where(used, stretch * one, 0.0)
            y_weight[term, half, 1] = jnp.where(
                used, viscosity * (stretch * stretch * two + bend * one), 0.0
            )

    along_z(1)
    over_ranks(lambda p: state_back(p, my_row).wait_recv())

    @pl.loop(0, length // LANES)
    def _(tile):
        at = lanes(tile * LANES)
        sums = [[[jnp.zeros((8, LANES), jnp.float32)] * 2 for _ in range(2)] for _ in range(3)]
        for term in range(16 + 6):
            for c in range(3):
                if term < 16:
                    row = v[c, term // 8, pl.ds(term % 8, 1), at]
                else:
                    row = s_back[c, pl.ds(term - 16, 1), at]
                for half in range(2):
                    sums[c][half] = [sums[c][half][i] + y_weight[term, half, i] * row for i in range(2)]
        for half in range(2):
            wind = v[1, half, :, at]
            for c in range(3):
                out[c, half, :, at] += sums[c][half][1] - wind * sums[c][half][0]

    def leave(half):
        return pltpu.make_async_copy(out.at[:, half], out_far.at[:, half], local_sem.at[6 + half])

    for half in range(2):
        over_planes(lambda p, half=half: back(half, p, my_plane).wait_recv())
        live = iota((8, LANES), 0) + 8 * half < count

        @pl.loop(0, length // LANES)
        def _(tile, half=half, live=live):
            at = lanes(tile * LANES)
            for c in range(3):
                out[c, half, :, at] = jnp.where(live, out[c, half, :, at] + z_back[c, half, :, at], 0.0)

        leave(half).start()

    for half in range(2):
        over_planes(lambda p, half=half: forth(half, my_plane, p).wait_send())
        over_planes(lambda p, half=half: back(half, my_plane, p).wait_send())
    over_ranks(lambda p: state_forth(my_row, p).wait_send())
    over_ranks(lambda p: state_back(my_row, p).wait_send())
    for half in range(2):
        leave(half).wait()


def local(ranks, planes, velocity, row_counts, y_metric, y_curvature):
    length = velocity.shape[3]
    live_total = y_metric.shape[0]
    z_cols, s_cols = length // planes, length // ranks
    far = pl.BlockSpec(memory_space=pltpu.HBM)
    whole = (3, 2, 8, length)
    line, plane = line_table().astype(np.float32), plane_table(planes).astype(np.float32)
    dma = pltpu.SemaphoreType.DMA
    f32, bf16 = jnp.float32, jnp.bfloat16
    result = pl.pallas_call(
        functools.partial(kernel, ranks, planes, live_total, length),
        out_shape=jax.ShapeDtypeStruct(whole, f32),
        in_specs=[far] * 6,
        out_specs=far,
        scratch_shapes=[
            pltpu.VMEM(whole, f32),
            pltpu.VMEM(whole, f32),
            pltpu.SMEM(row_counts.shape, jnp.int32),
            pltpu.SMEM(y_metric.shape, f32),
            pltpu.SMEM(y_curvature.shape, f32),
            pltpu.VMEM(line.shape, f32),
            pltpu.VMEM(plane.shape, f32),
            pltpu.VMEM(line.shape, bf16),
            pltpu.VMEM(line.shape, bf16),
            pltpu.VMEM(plane.shape, bf16),
            pltpu.VMEM(plane.shape, bf16),
            pltpu.VMEM((ranks * STATES, ranks * STATES), f32),
            pltpu.VMEM((48, length + LANES), bf16),
            pltpu.VMEM((48, length + LANES), bf16),
            pltpu.VMEM((2, planes, 3, 8, z_cols), f32),
            pltpu.VMEM((2, planes, 3, 8, z_cols), f32),
            pltpu.VMEM(whole, f32),
            pltpu.VMEM((3, STATES, length), f32),
            pltpu.VMEM((ranks, 3, STATES, s_cols), f32),
            pltpu.VMEM((ranks, 3, STATES, s_cols), f32),
            pltpu.VMEM((3, STATES, length), f32),
            pltpu.VMEM((16, STATES, LANES), f32),
            pltpu.VMEM((22, 2, 2, 8, LANES), f32),
            dma((8,)),
            dma((2, planes)),
            dma((2, planes)),
            dma((2, planes)),
            dma((2, planes)),
            dma((ranks,)),
            dma((ranks,)),
            dma((ranks,)),
            dma((ranks,)),
        ],
        compiler_params=pltpu.CompilerParams(
            collective_id=0, has_side_effects=True, vmem_limit_bytes=63 * 1024 * 1024
        ),
        cost_estimate=pl.CostEstimate(flops=10**9, bytes_accessed=2 * 10**6, transcendentals=10**5),
    )(velocity.reshape(whole), row_counts, y_metric, y_curvature, jnp.asarray(line), jnp.asarray(plane))
    return result.reshape(velocity.shape)


def solution(mesh):
    return jax.shard_map(
        functools.partial(local, mesh.shape["row"], mesh.shape["span"]),
        mesh=mesh,
        in_specs=(P(None, "span", "row", None), P(), P(), P()),
        out_specs=P(None, "span", "row", None),
        check_vma=False,
    )
```

```python
import functools
import math

import jax
import jax.numpy as jnp
import numpy as np
from jax import lax
from jax.experimental import pallas as pl
from jax.experimental.pallas import tpu as pltpu
from jax.sharding import PartitionSpec as P

MESH = pl.DeviceIdType.MESH
viscosity = 0.2
LANES = 128
STATES = 8


def scheme(alpha, first):
    root = math.sqrt(1.0 - 4.0 * alpha * alpha)
    decay = (1.0 - root) / (2.0 * alpha)

    def res(s):
        return (-decay) ** abs(s) / root

    def tap(s):
        if first:
            return 0.5 * 14.0 / 9.0 * (res(s - 1) - res(s + 1)) + 0.25 / 9.0 * (res(s - 2) - res(s + 2))
        return (
            12.0 / 11.0 * (res(s - 1) - 2.0 * res(s) + res(s + 1))
            + 0.25 * 3.0 / 11.0 * (res(s - 2) - 2.0 * res(s) + res(s + 2))
        )

    amp = tap(2) / decay**2
    return dict(tap=tap, log=math.log(decay), amp=amp, near=tap(1) + amp * decay, centre=tap(0))


FIRST = scheme(1.0 / 3.0, True)
SECOND = scheme(2.0 / 11.0, False)


def line_table():
    table = np.zeros((2 * LANES, 2 * LANES))
    for p in range(2 * LANES):
        for q in range(LANES):
            shift = p - LANES // 2 - q
            table[p, q] = FIRST["tap"](shift)
            table[p, LANES + q] = viscosity * SECOND["tap"](shift)
    return table


def plane_table(count):
    table = np.zeros((2, count, 8, count, 8))
    for m in range(count):
        for n in range(count):
            for turn in range(-40, 41):
                shift = n - m + turn * count
                for row in range(8):
                    table[0, m, row, n, row] += FIRST["tap"](shift)
                    table[1, m, row, n, row] += viscosity * SECOND["tap"](shift)
    return table.reshape(16 * count, 8 * count)


def split(values):
    high = values.astype(jnp.bfloat16)
    return high, (values - high.astype(jnp.float32)).astype(jnp.bfloat16)


def product(left, right):
    dot = functools.partial(jnp.dot, preferred_element_type=jnp.float32)
    return dot(left[0], right[0]) + (dot(left[0], right[1]) + dot(left[1], right[0]))


def power(log, steps):
    size = jnp.exp(steps.astype(jnp.float32) * log)
    return jnp.where(steps % 2 == 0, size, -size)


def iota(shape, axis):
    return lax.broadcasted_iota(jnp.int32, shape, axis)


def partner(index, me, count):
    half = count // 2
    step = jnp.where(index % 2 == 1, half - (index + 1) // 2, half + index // 2)
    return (me + step) % count


def kernel(
    ranks, planes, live_total, length,
    v_far, counts_far, metric_far, curvature_far, line_far, plane_far,
    out_far,
    out, v, counts, metric, curvature, line, plane, line_high, line_low, plane_high, plane_low, matrix,
    pad_high, pad_low, z_in, z_out, z_back, relay, s_out, s_in, s_mid, s_back, s_weight, y_weight,
    local_sem, z_send, z_recv, zb_send, zb_recv, s_send, s_recv, sb_send, sb_recv, relay_sem,
):
    my_row, my_plane = lax.axis_index("row"), lax.axis_index("span")
    z_cols, s_cols = length // planes, length // ranks

    def lanes(start, size=LANES):
        return pl.ds(pl.multiple_of(start, LANES), size)

    def forth(half, source, target):
        return pltpu.make_async_remote_copy(
            src_ref=v_far.at[:, half, :, lanes(target * z_cols, z_cols)],
            dst_ref=z_in.at[half, source],
            send_sem=z_send.at[half, target],
            recv_sem=z_recv.at[half, source],
            device_id={"span": target},
            device_id_type=MESH,
        )

    def back(half, source, target):
        return pltpu.make_async_remote_copy(
            src_ref=z_out.at[half, target],
            dst_ref=z_back.at[:, half, :, lanes(source * z_cols, z_cols)],
            send_sem=zb_send.at[half, target],
            recv_sem=zb_recv.at[half, source],
            device_id={"span": target},
            device_id_type=MESH,
        )

    def state_forth(source, target):
        return pltpu.make_async_remote_copy(
            src_ref=s_out.at[:, :, lanes(target * s_cols, s_cols)],
            dst_ref=s_in.at[source],
            send_sem=s_send.at[target],
            recv_sem=s_recv.at[source],
            device_id={"row": target},
            device_id_type=MESH,
        )

    def state_back(source, target):
        return pltpu.make_async_remote_copy(
            src_ref=s_mid.at[target],
            dst_ref=s_back.at[:, :, lanes(source * s_cols, s_cols)],
            send_sem=sb_send.at[target],
            recv_sem=sb_recv.at[source],
            device_id={"row": target},
            device_id_type=MESH,
        )

    def over_planes(act):
        pl.loop(0, planes - 1)(lambda index: act(partner(index, my_plane, planes)))

    chips = planes // 2
    reach = chips // 2
    near = 4 * (reach - 1) + 1
    my_chip, my_core = my_plane // 2, my_plane % 2

    def over_near(act):
        @pl.loop(0, near)
        def _(index):
            away = reach - 1 - index // 4
            chip = jnp.where(index % 2 == 0, my_chip + away, my_chip + chips - away) % chips
            act(chip * 2 + jnp.where(index == near - 1, 1 - my_core, index // 2 % 2))

    def flip(place):
        return place + 1 - 2 * (place % 2)

    ahead_plane, behind_plane = (my_plane + reach) % planes, (my_plane + planes - reach) % planes
    relays = [ahead_plane, behind_plane]
    opposite = (my_plane + chips) % planes
    finals = [opposite, flip(opposite)]
    origins, goals = [behind_plane, ahead_plane], [ahead_plane, flip(behind_plane)]

    def relay_copy(held, leg, half, way, src, dst, target):
        sems = relay_sem.at[held, leg, half, way], relay_sem.at[held, 1, half, way]
        return pltpu.make_async_remote_copy(
            src, dst, sems[0], sems[1], device_id={"span": target}, device_id_type=MESH
        )

    def forth_first(half, way):
        src = v_far.at[:, half, :, lanes(finals[way] * z_cols, z_cols)]
        return relay_copy(0, 0, half, way, src, relay.at[0, half, way], relays[way])

    def back_first(half, way):
        return relay_copy(1, 0, half, way, z_out.at[half, finals[way]], relay.at[1, half, way], relays[way])

    def forth_second(half, way):
        return pltpu.make_async_remote_copy(
            src_ref=relay.at[0, half, way],
            dst_ref=z_in.at[half, origins[way]],
            send_sem=relay_sem.at[0, 2, half, way],
            recv_sem=z_recv.at[half, origins[way]],
            device_id={"span": goals[way]},
            device_id_type=MESH,
        )

    def back_second(half, way):
        return pltpu.make_async_remote_copy(
            src_ref=relay.at[1, half, way],
            dst_ref=z_back.at[:, half, :, lanes(origins[way] * z_cols, z_cols)],
            send_sem=relay_sem.at[1, 2, half, way],
            recv_sem=zb_recv.at[half, origins[way]],
            device_id={"span": goals[way]},
            device_id_type=MESH,
        )

    def send(first, direct, half):
        for way in range(2):
            first(half, way).start()
        over_near(lambda p: direct(half, my_plane, p).start())

    def pass_on(first, second, half):
        for way in range(2):
            first(half, way).wait_recv()
            second(half, way).start()

    def sent(first, second, direct, half):
        for way in range(2):
            first(half, way).wait_send()
            second(half, way).wait_send()
        over_near(lambda p: direct(half, my_plane, p).wait_send())

    def over_ranks(act):
        pl.loop(0, ranks - 1)(lambda index: act(partner(index, my_row, ranks)))

    barrier = pltpu.get_barrier_semaphore()
    over_planes(lambda p: pl.semaphore_signal(barrier, 1, device_id={"span": p}, device_id_type=MESH))
    over_ranks(lambda p: pl.semaphore_signal(barrier, 1, device_id={"row": p}, device_id_type=MESH))
    pairs = [(counts_far, counts), (v_far, v), (metric_far, metric), (curvature_far, curvature)]
    pairs += [(line_far, line), (plane_far, plane)]
    copies = [pltpu.make_async_copy(*pair, local_sem.at[i]) for i, pair in enumerate(pairs)]
    for copy in copies:
        copy.start()

    copies[0].wait()
    count = counts[my_row]
    kind = iota((STATES, LANES), 0)
    decay_log = jnp.where(kind % 2 == 0, FIRST["log"], SECOND["log"])
    for k in range(16):
        steps = jnp.where(kind < 2, jnp.maximum(count - 1 - k, 0), k)
        weight = jnp.where(kind < 4, power(decay_log, steps), 0.0)
        weight = jnp.where((kind == 4) & (k == 0), 1.0, weight)
        weight = jnp.where((kind == 5) & (count - 1 == k), 1.0, weight)
        s_weight[k] = jnp.where(k < count, weight, 0.0)

    pl.semaphore_wait(barrier, planes + ranks - 2)
    send(forth_first, forth, 0)
    copies[1].wait()

    @pl.loop(0, length // LANES)
    def _(tile):
        at = lanes(tile * LANES)
        totals = [jnp.zeros((STATES, LANES), jnp.float32)] * 3
        for k in range(16):
            weight = s_weight[k]
            totals = [totals[c] + weight * v[c, k // 8, pl.ds(k % 8, 1), at] for c in range(3)]
        for c in range(3):
            s_out[c, :, at] = totals[c]

    over_ranks(lambda p: state_forth(my_row, p).start())
    send(forth_first, forth, 1)
    s_in[my_row] = s_out[:, :, lanes(my_row * s_cols, s_cols)]
    for half in range(2):
        z_in[half, my_plane] = v[:, half, :, lanes(my_plane * z_cols, z_cols)]

    pass_on(forth_first, forth_second, 0)
    for copy in copies[2:]:
        copy.wait()
    line_high[...], line_low[...] = split(line[...])
    plane_high[...], plane_low[...] = split(plane[...])

    for c in range(3):
        turned = pltpu.roll(v[c].reshape(16, length), LANES // 2, 1)
        high, low = split(turned)
        rows = pl.ds(16 * c, 16)
        pad_high[rows, pl.ds(0, length)] = high
        pad_low[rows, pl.ds(0, length)] = low
        pad_high[rows, pl.ds(length, LANES)] = high[:, :LANES]
        pad_low[rows, pl.ds(length, LANES)] = low[:, :LANES]

    group = 4

    @pl.loop(0, length // (LANES * group))
    def _(step):
        def windows(ref):
            return jnp.concatenate(
                [ref[:, lanes((step * group + i) * LANES, 2 * LANES)] for i in range(group)], axis=0
            )

        both = product((windows(pad_high), windows(pad_low)), (line_high[...], line_low[...]))
        for i in range(group):
            at = lanes((step * group + i) * LANES)
            wind = v[0, :, :, at].reshape(16, LANES)
            for c in range(3):
                rows = slice(48 * i + 16 * c, 48 * i + 16 * c + 16)
                part = both[rows, LANES:] - wind * both[rows, :LANES]
                out[c, :, :, at] = part.reshape(2, 8, LANES)

    def along_z(half):
        over_planes(lambda p: forth(half, p, my_plane).wait_recv())
        for part in range(z_cols // LANES):
            cut = slice(part * LANES, (part + 1) * LANES)
            held = [z_in[half, :, c, :, cut].reshape(8 * planes, LANES) for c in range(3)]
            both = product((plane_high[...], plane_low[...]), split(jnp.concatenate(held, axis=1)))
            for c in range(3):
                at = slice(c * LANES, (c + 1) * LANES)
                term = both[8 * planes :, at] - held[2] * both[: 8 * planes, at]
                z_out[half, :, c, :, cut] = term.reshape(planes, 8, LANES)
        send(back_first, back, half)
        z_back[:, half, :, lanes(my_plane * z_cols, z_cols)] = z_out[half, my_plane]

    size = ranks * STATES
    col_rank, col_kind = iota((8, size), 1) // STATES, iota((8, size), 1) % STATES
    row_kind = iota((8, size), 0)
    row_log = jnp.where(row_kind % 2 == 0, FIRST["log"], SECOND["log"])
    col_start = col_count = jnp.zeros((8, size), jnp.int32)
    start = jnp.int32(0)
    for rank in range(ranks):
        col_start = col_start + jnp.where(rank < col_rank, counts[rank], 0)
        col_count = jnp.where(rank == col_rank, counts[rank], col_count)
        start = start + jnp.where(rank < my_row, counts[rank], 0)

    def rank_rows(rank, row_start):
        row_count = counts[rank]
        ahead = row_start - col_start - col_count
        ahead = jnp.where(ahead < 0, ahead + live_total, ahead)
        behind = col_start - row_start - row_count
        behind = jnp.where(behind < 0, behind + live_total, behind)
        same = power(row_log, jnp.where(row_kind < 2, ahead, behind))
        rows = jnp.where((row_kind == col_kind) & (row_kind < 4), same, 0.0)
        rows = jnp.where((row_kind == 4) & (col_kind == 5) & (ahead == 0), 1.0, rows)
        rows = jnp.where((row_kind == 5) & (col_kind == 4) & (behind == 0), 1.0, rows)
        matrix[pl.ds(pl.multiple_of(rank * STATES, STATES), STATES), :] = rows
        return row_start + row_count

    lax.fori_loop(0, ranks, rank_rows, jnp.int32(0))

    def over_y():
        over_ranks(lambda p: state_forth(p, my_row).wait_recv())
        held = [s_in[:, c].reshape(size, s_cols) for c in range(3)]
        both = product(split(matrix[...]), split(jnp.concatenate(held, axis=1)))
        for c in range(3):
            s_mid[:, c] = both[:, c * s_cols : (c + 1) * s_cols].reshape(ranks, STATES, s_cols)
        over_ranks(lambda p: state_back(my_row, p).start())
        s_back[:, :, lanes(my_row * s_cols, s_cols)] = s_mid[my_row]

    pass_on(forth_first, forth_second, 1)
    along_z(0)
    over_y()
    pass_on(back_first, back_second, 0)

    for half in range(2):
        slot = iota((8, LANES), 0) + 8 * half
        stretch = jnp.zeros((8, LANES), jnp.float32)
        bend = jnp.zeros((8, LANES), jnp.float32)
        for k in range(8 * half, 8 * half + 8):
            grid_row = jnp.minimum(start + k, live_total - 1)
            stretch = jnp.where(slot == k, metric[grid_row], stretch)
            bend = jnp.where(slot == k, curvature[grid_row], bend)
        live = slot < count
        tail = jnp.maximum(count - slot, 0)
        for term in range(16 + 6):
            if term < 16:
                away = jnp.abs(term - slot)
                one = FIRST["amp"] * power(FIRST["log"], away) + jnp.where(away == 1, FIRST["near"], 0.0)
                one = jnp.where(away == 0, 0.0, jnp.where(term > slot, one, -one))
                two = SECOND["amp"] * power(SECOND["log"], away) + jnp.where(away == 1, SECOND["near"], 0.0)
                two = jnp.where(away == 0, SECOND["centre"], two)
                used = live & (term < count)
            else:
                one = two = jnp.zeros((8, LANES), jnp.float32)
                used = live
                if term == 16:
                    one = -FIRST["amp"] * power(FIRST["log"], slot + 1)
                if term == 17:
                    two = SECOND["amp"] * power(SECOND["log"], slot + 1)
                if term == 18:
                    one = FIRST["amp"] * power(FIRST["log"], tail)
                if term == 19:
                    two = SECOND["amp"] * power(SECOND["log"], tail)
                if term == 20:
                    one = jnp.where(slot == 0, -FIRST["near"], 0.0)
                    two = jnp.where(slot == 0, SECOND["near"], 0.0)
                if term == 21:
                    one = jnp.where(tail == 1, FIRST["near"], 0.0)
                    two = jnp.where(tail == 1, SECOND["near"], 0.0)
            y_weight[term, half, 0] = jnp.where(used, stretch * one, 0.0)
            y_weight[term, half, 1] = jnp.where(
                used, viscosity * (stretch * stretch * two + bend * one), 0.0
            )

    along_z(1)
    over_ranks(lambda p: state_back(p, my_row).wait_recv())

    def along_y(tile):
        at = lanes(tile * LANES)
        sums = [[[jnp.zeros((8, LANES), jnp.float32)] * 2 for _ in range(2)] for _ in range(3)]
        for term in range(16 + 6):
            for c in range(3):
                if term < 16:
                    row = v[c, term // 8, pl.ds(term % 8, 1), at]
                else:
                    row = s_back[c, pl.ds(term - 16, 1), at]
                for half in range(2):
                    sums[c][half] = [sums[c][half][i] + y_weight[term, half, i] * row for i in range(2)]
        for half in range(2):
            wind = v[1, half, :, at]
            for c in range(3):
                out[c, half, :, at] += sums[c][half][1] - wind * sums[c][half][0]

    tiles = length // LANES
    pl.loop(0, tiles // 2)(along_y)
    pass_on(back_first, back_second, 1)
    pl.loop(tiles // 2, tiles)(along_y)
    for half in range(2):
        sent(forth_first, forth_second, forth, half)
    over_ranks(lambda p: state_forth(my_row, p).wait_send())
    over_ranks(lambda p: state_back(my_row, p).wait_send())
    sent(back_first, back_second, back, 0)

    def leave(half):
        return pltpu.make_async_copy(out.at[:, half], out_far.at[:, half], local_sem.at[6 + half])

    for half in range(2):
        over_planes(lambda p, half=half: back(half, p, my_plane).wait_recv())
        live = iota((8, LANES), 0) + 8 * half < count

        @pl.loop(0, length // LANES)
        def _(tile, half=half, live=live):
            at = lanes(tile * LANES)
            for c in range(3):
                out[c, half, :, at] = jnp.where(live, out[c, half, :, at] + z_back[c, half, :, at], 0.0)

        leave(half).start()

    sent(back_first, back_second, back, 1)
    for half in range(2):
        leave(half).wait()


def local(ranks, planes, velocity, row_counts, y_metric, y_curvature):
    length = velocity.shape[3]
    live_total = y_metric.shape[0]
    z_cols, s_cols = length // planes, length // ranks
    far = pl.BlockSpec(memory_space=pltpu.HBM)
    whole = (3, 2, 8, length)
    line, plane = line_table().astype(np.float32), plane_table(planes).astype(np.float32)
    dma = pltpu.SemaphoreType.DMA
    f32, bf16 = jnp.float32, jnp.bfloat16
    result = pl.pallas_call(
        functools.partial(kernel, ranks, planes, live_total, length),
        out_shape=jax.ShapeDtypeStruct(whole, f32),
        in_specs=[far] * 6,
        out_specs=far,
        scratch_shapes=[
            pltpu.VMEM(whole, f32),
            pltpu.VMEM(whole, f32),
            pltpu.SMEM(row_counts.shape, jnp.int32),
            pltpu.SMEM(y_metric.shape, f32),
            pltpu.SMEM(y_curvature.shape, f32),
            pltpu.VMEM(line.shape, f32),
            pltpu.VMEM(plane.shape, f32),
            pltpu.VMEM(line.shape, bf16),
            pltpu.VMEM(line.shape, bf16),
            pltpu.VMEM(plane.shape, bf16),
            pltpu.VMEM(plane.shape, bf16),
            pltpu.VMEM((ranks * STATES, ranks * STATES), f32),
            pltpu.VMEM((48, length + LANES), bf16),
            pltpu.VMEM((48, length + LANES), bf16),
            pltpu.VMEM((2, planes, 3, 8, z_cols), f32),
            pltpu.VMEM((2, planes, 3, 8, z_cols), f32),
            pltpu.VMEM(whole, f32),
            pltpu.VMEM((2, 2, 2, 3, 8, z_cols), f32),
            pltpu.VMEM((3, STATES, length), f32),
            pltpu.VMEM((ranks, 3, STATES, s_cols), f32),
            pltpu.VMEM((ranks, 3, STATES, s_cols), f32),
            pltpu.VMEM((3, STATES, length), f32),
            pltpu.VMEM((16, STATES, LANES), f32),
            pltpu.VMEM((22, 2, 2, 8, LANES), f32),
            dma((8,)),
            dma((2, planes)),
            dma((2, planes)),
            dma((2, planes)),
            dma((2, planes)),
            dma((ranks,)),
            dma((ranks,)),
            dma((ranks,)),
            dma((ranks,)),
            dma((2, 3, 2, 2)),
        ],
        compiler_params=pltpu.CompilerParams(
            collective_id=0, has_side_effects=True, vmem_limit_bytes=63 * 1024 * 1024
        ),
        cost_estimate=pl.CostEstimate(flops=10**9, bytes_accessed=2 * 10**6, transcendentals=10**5),
    )(velocity.reshape(whole), row_counts, y_metric, y_curvature, jnp.asarray(line), jnp.asarray(plane))
    return result.reshape(velocity.shape)


def solution(mesh):
    return jax.shard_map(
        functools.partial(local, mesh.shape["row"], mesh.shape["span"]),
        mesh=mesh,
        in_specs=(P(None, "span", "row", None), P(), P(), P()),
        out_specs=P(None, "span", "row", None),
        check_vma=False,
    )
```

```python
import functools
import math

import jax
import jax.numpy as jnp
import numpy as np
from jax import lax
from jax.experimental import pallas as pl
from jax.experimental.pallas import tpu as pltpu
from jax.sharding import PartitionSpec as P

MESH = pl.DeviceIdType.MESH
viscosity = 0.2
LANES = 128
STATES = 8


def scheme(alpha, first):
    root = math.sqrt(1.0 - 4.0 * alpha * alpha)
    decay = (1.0 - root) / (2.0 * alpha)

    def res(s):
        return (-decay) ** abs(s) / root

    def tap(s):
        if first:
            return 0.5 * 14.0 / 9.0 * (res(s - 1) - res(s + 1)) + 0.25 / 9.0 * (res(s - 2) - res(s + 2))
        return (
            12.0 / 11.0 * (res(s - 1) - 2.0 * res(s) + res(s + 1))
            + 0.25 * 3.0 / 11.0 * (res(s - 2) - 2.0 * res(s) + res(s + 2))
        )

    amp = tap(2) / decay**2
    return dict(tap=tap, log=math.log(decay), amp=amp, near=tap(1) + amp * decay, centre=tap(0))


FIRST = scheme(1.0 / 3.0, True)
SECOND = scheme(2.0 / 11.0, False)


def line_table():
    table = np.zeros((2 * LANES, 2 * LANES))
    for p in range(2 * LANES):
        for q in range(LANES):
            shift = p - LANES // 2 - q
            table[p, q] = FIRST["tap"](shift)
            table[p, LANES + q] = viscosity * SECOND["tap"](shift)
    return table


def plane_table(count):
    table = np.zeros((2, count, 8, count, 8))
    for m in range(count):
        for n in range(count):
            for turn in range(-40, 41):
                shift = n - m + turn * count
                for row in range(8):
                    table[0, m, row, n, row] += FIRST["tap"](shift)
                    table[1, m, row, n, row] += viscosity * SECOND["tap"](shift)
    return table.reshape(16 * count, 8 * count)


def split(values):
    high = values.astype(jnp.bfloat16)
    return high, (values - high.astype(jnp.float32)).astype(jnp.bfloat16)


def product(left, right):
    dot = functools.partial(jnp.dot, preferred_element_type=jnp.float32)
    return dot(left[0], right[0]) + (dot(left[0], right[1]) + dot(left[1], right[0]))


def power(log, steps):
    size = jnp.exp(steps.astype(jnp.float32) * log)
    return jnp.where(steps % 2 == 0, size, -size)


def iota(shape, axis):
    return lax.broadcasted_iota(jnp.int32, shape, axis)


def partner(index, me, count):
    half = count // 2
    step = jnp.where(index % 2 == 1, half - (index + 1) // 2, half + index // 2)
    return (me + step) % count


def kernel(
    ranks, planes, live_total, length,
    v_far, counts_far, metric_far, curvature_far, line_far, plane_far,
    out_far, z_back,
    out, v, counts, metric, curvature, line, plane, line_high, line_low, plane_high, plane_low, matrix,
    pad_high, pad_low, z_in, z_out, s_out, s_in, s_mid, s_back, s_weight, y_weight,
    local_sem, z_send, z_recv, zb_send, zb_recv, s_send, s_recv, sb_send, sb_recv,
):
    my_row, my_plane = lax.axis_index("row"), lax.axis_index("span")
    z_cols, s_cols = length // planes, length // ranks

    def lanes(start, size=LANES):
        return pl.ds(pl.multiple_of(start, LANES), size)

    def forth(half, source, target):
        return pltpu.make_async_remote_copy(
            src_ref=v_far.at[:, half, :, lanes(target * z_cols, z_cols)],
            dst_ref=z_in.at[half, source],
            send_sem=z_send.at[half, target],
            recv_sem=z_recv.at[half, source],
            device_id={"span": target},
            device_id_type=MESH,
        )

    def back(half, source, target):
        return pltpu.make_async_remote_copy(
            src_ref=z_out.at[half, target],
            dst_ref=z_back.at[:, half, :, lanes(source * z_cols, z_cols)],
            send_sem=zb_send.at[half, target],
            recv_sem=zb_recv.at[half, source],
            device_id={"span": target},
            device_id_type=MESH,
        )

    def state_forth(source, target):
        return pltpu.make_async_remote_copy(
            src_ref=s_out.at[:, :, lanes(target * s_cols, s_cols)],
            dst_ref=s_in.at[source],
            send_sem=s_send.at[target],
            recv_sem=s_recv.at[source],
            device_id={"row": target},
            device_id_type=MESH,
        )

    def state_back(source, target):
        return pltpu.make_async_remote_copy(
            src_ref=s_mid.at[target],
            dst_ref=s_back.at[:, :, lanes(source * s_cols, s_cols)],
            send_sem=sb_send.at[target],
            recv_sem=sb_recv.at[source],
            device_id={"row": target},
            device_id_type=MESH,
        )

    def over_planes(act):
        pl.loop(0, planes - 1)(lambda index: act(partner(index, my_plane, planes)))

    def over_ranks(act):
        pl.loop(0, ranks - 1)(lambda index: act(partner(index, my_row, ranks)))

    barrier = pltpu.get_barrier_semaphore()
    over_planes(lambda p: pl.semaphore_signal(barrier, 1, device_id={"span": p}, device_id_type=MESH))
    over_ranks(lambda p: pl.semaphore_signal(barrier, 1, device_id={"row": p}, device_id_type=MESH))
    pairs = [(counts_far, counts), (v_far, v), (metric_far, metric), (curvature_far, curvature)]
    pairs += [(line_far, line), (plane_far, plane)]
    copies = [pltpu.make_async_copy(*pair, local_sem.at[i]) for i, pair in enumerate(pairs)]
    for copy in copies:
        copy.start()

    copies[0].wait()
    count = counts[my_row]
    kind = iota((STATES, LANES), 0)
    decay_log = jnp.where(kind % 2 == 0, FIRST["log"], SECOND["log"])
    for k in range(16):
        steps = jnp.where(kind < 2, jnp.maximum(count - 1 - k, 0), k)
        weight = jnp.where(kind < 4, power(decay_log, steps), 0.0)
        weight = jnp.where((kind == 4) & (k == 0), 1.0, weight)
        weight = jnp.where((kind == 5) & (count - 1 == k), 1.0, weight)
        s_weight[k] = jnp.where(k < count, weight, 0.0)

    pl.semaphore_wait(barrier, planes + ranks - 2)
    for half in range(2):
        over_planes(lambda p, half=half: forth(half, my_plane, p).start())
    copies[1].wait()

    @pl.loop(0, length // LANES, unroll=2)
    def _(tile):
        at = lanes(tile * LANES)
        totals = [jnp.zeros((STATES, LANES), jnp.float32)] * 3
        for k in range(16):
            weight = s_weight[k]
            totals = [totals[c] + weight * v[c, k // 8, pl.ds(k % 8, 1), at] for c in range(3)]
        for c in range(3):
            s_out[c, :, at] = totals[c]

    over_ranks(lambda p: state_forth(my_row, p).start())
    s_in[my_row] = s_out[:, :, lanes(my_row * s_cols, s_cols)]
    for half in range(2):
        z_in[half, my_plane] = v[:, half, :, lanes(my_plane * z_cols, z_cols)]

    for copy in copies[2:]:
        copy.wait()
    line_high[...], line_low[...] = split(line[...])
    plane_high[...], plane_low[...] = split(plane[...])

    for c in range(3):
        turned = pltpu.roll(v[c].reshape(16, length), LANES // 2, 1)
        high, low = split(turned)
        rows = pl.ds(16 * c, 16)
        pad_high[rows, pl.ds(0, length)] = high
        pad_low[rows, pl.ds(0, length)] = low
        pad_high[rows, pl.ds(length, LANES)] = high[:, :LANES]
        pad_low[rows, pl.ds(length, LANES)] = low[:, :LANES]

    group = 8

    def along_x(step):
        def windows(ref):
            return jnp.concatenate(
                [ref[:, lanes((step * group + i) * LANES, 2 * LANES)] for i in range(group)], axis=0
            )

        both = product((windows(pad_high), windows(pad_low)), (line_high[...], line_low[...]))
        for i in range(group):
            at = lanes((step * group + i) * LANES)
            wind = v[0, :, :, at].reshape(16, LANES)
            for c in range(3):
                rows = slice(48 * i + 16 * c, 48 * i + 16 * c + 16)
                part = both[rows, LANES:] - wind * both[rows, :LANES]
                out[c, :, :, at] = part.reshape(2, 8, LANES)

    def keep(half):
        own = z_back.at[:, half, :, lanes(my_plane * z_cols, z_cols)]
        return pltpu.make_async_copy(z_out.at[half, my_plane], own, local_sem.at[7 + half])

    def along_z(half):
        over_planes(lambda p: forth(half, p, my_plane).wait_recv())
        live = iota((planes, 8, LANES), 1) + 8 * half < count
        for part in range(z_cols // LANES):
            cut = slice(part * LANES, (part + 1) * LANES)
            held = [z_in[half, :, c, :, cut].reshape(8 * planes, LANES) for c in range(3)]
            both = product((plane_high[...], plane_low[...]), split(jnp.concatenate(held, axis=1)))
            for c in range(3):
                at = slice(c * LANES, (c + 1) * LANES)
                term = both[8 * planes :, at] - held[2] * both[: 8 * planes, at]
                z_out[half, :, c, :, cut] = jnp.where(live, term.reshape(planes, 8, LANES), 0.0)
        over_planes(lambda p: back(half, my_plane, p).start())
        keep(half).start()

    pl.loop(0, length // (LANES * group))(along_x)

    size = ranks * STATES
    col_rank, col_kind = iota((8, size), 1) // STATES, iota((8, size), 1) % STATES
    row_kind = iota((8, size), 0)
    row_log = jnp.where(row_kind % 2 == 0, FIRST["log"], SECOND["log"])
    col_start = col_count = jnp.zeros((8, size), jnp.int32)
    start = jnp.int32(0)
    for rank in range(ranks):
        col_start = col_start + jnp.where(rank < col_rank, counts[rank], 0)
        col_count = jnp.where(rank == col_rank, counts[rank], col_count)
        start = start + jnp.where(rank < my_row, counts[rank], 0)

    def rank_rows(rank, row_start):
        row_count = counts[rank]
        ahead = row_start - col_start - col_count
        ahead = jnp.where(ahead < 0, ahead + live_total, ahead)
        behind = col_start - row_start - row_count
        behind = jnp.where(behind < 0, behind + live_total, behind)
        same = power(row_log, jnp.where(row_kind < 2, ahead, behind))
        rows = jnp.where((row_kind == col_kind) & (row_kind < 4), same, 0.0)
        rows = jnp.where((row_kind == 4) & (col_kind == 5) & (ahead == 0), 1.0, rows)
        rows = jnp.where((row_kind == 5) & (col_kind == 4) & (behind == 0), 1.0, rows)
        matrix[pl.ds(pl.multiple_of(rank * STATES, STATES), STATES), :] = rows
        return row_start + row_count

    lax.fori_loop(0, ranks, rank_rows, jnp.int32(0), unroll=4)

    def over_y():
        over_ranks(lambda p: state_forth(p, my_row).wait_recv())
        held = [s_in[:, c].reshape(size, s_cols) for c in range(3)]
        both = product(split(matrix[...]), split(jnp.concatenate(held, axis=1)))
        for c in range(3):
            s_mid[:, c] = both[:, c * s_cols : (c + 1) * s_cols].reshape(ranks, STATES, s_cols)
        over_ranks(lambda p: state_back(my_row, p).start())
        s_back[:, :, lanes(my_row * s_cols, s_cols)] = s_mid[my_row]

    for half in range(2):
        slot = iota((8, LANES), 0) + 8 * half
        stretch = jnp.zeros((8, LANES), jnp.float32)
        bend = jnp.zeros((8, LANES), jnp.float32)
        for k in range(8 * half, 8 * half + 8):
            grid_row = jnp.minimum(start + k, live_total - 1)
            stretch = jnp.where(slot == k, metric[grid_row], stretch)
            bend = jnp.where(slot == k, curvature[grid_row], bend)
        live = slot < count
        tail = jnp.maximum(count - slot, 0)
        for term in range(16 + 6):
            if term < 16:
                away = jnp.abs(term - slot)
                one = FIRST["amp"] * power(FIRST["log"], away) + jnp.where(away == 1, FIRST["near"], 0.0)
                one = jnp.where(away == 0, 0.0, jnp.where(term > slot, one, -one))
                two = SECOND["amp"] * power(SECOND["log"], away) + jnp.where(away == 1, SECOND["near"], 0.0)
                two = jnp.where(away == 0, SECOND["centre"], two)
                used = live & (term < count)
            else:
                one = two = jnp.zeros((8, LANES), jnp.float32)
                used = live
                if term == 16:
                    one = -FIRST["amp"] * power(FIRST["log"], slot + 1)
                if term == 17:
                    two = SECOND["amp"] * power(SECOND["log"], slot + 1)
                if term == 18:
                    one = FIRST["amp"] * power(FIRST["log"], tail)
                if term == 19:
                    two = SECOND["amp"] * power(SECOND["log"], tail)
                if term == 20:
                    one = jnp.where(slot == 0, -FIRST["near"], 0.0)
                    two = jnp.where(slot == 0, SECOND["near"], 0.0)
                if term == 21:
                    one = jnp.where(tail == 1, FIRST["near"], 0.0)
                    two = jnp.where(tail == 1, SECOND["near"], 0.0)
            y_weight[term, half, 0] = jnp.where(used, stretch * one, 0.0)
            y_weight[term, half, 1] = jnp.where(
                used, viscosity * (stretch * stretch * two + bend * one), 0.0
            )

    along_z(0)
    along_z(1)
    over_y()
    for half in range(2):
        over_planes(lambda p, half=half: forth(half, my_plane, p).wait_send())
    over_ranks(lambda p: state_forth(my_row, p).wait_send())
    over_ranks(lambda p: state_back(p, my_row).wait_recv())

    def along_y(tile):
        at = lanes(tile * LANES)
        sums = [[[jnp.zeros((8, LANES), jnp.float32)] * 2 for _ in range(2)] for _ in range(3)]
        for term in range(16 + 6):
            for c in range(3):
                if term < 16:
                    row = v[c, term // 8, pl.ds(term % 8, 1), at]
                else:
                    row = s_back[c, pl.ds(term - 16, 1), at]
                for half in range(2):
                    sums[c][half] = [sums[c][half][i] + y_weight[term, half, i] * row for i in range(2)]
        for half in range(2):
            wind = v[1, half, :, at]
            live = iota((8, LANES), 0) + 8 * half < count
            for c in range(3):
                term = out[c, half, :, at] + sums[c][half][1] - wind * sums[c][half][0]
                out[c, half, :, at] = jnp.where(live, term, 0.0)

    pl.loop(0, length // LANES)(along_y)
    leave = pltpu.make_async_copy(out, out_far, local_sem.at[6])
    leave.start()
    over_ranks(lambda p: state_back(my_row, p).wait_send())
    for half in range(2):
        over_planes(lambda p, half=half: back(half, my_plane, p).wait_send())
    for half in range(2):
        over_planes(lambda p, half=half: back(half, p, my_plane).wait_recv())
        keep(half).wait()
    leave.wait()


def add_kernel(left_far, right_far, out_far, left, right, load_sem, store_sem):
    def load(c, i):
        return pltpu.make_async_copy((left_far, right_far)[i].at[c], (left, right)[i].at[c], load_sem.at[c, i])

    def store(c):
        return pltpu.make_async_copy(left.at[c], out_far.at[c], store_sem.at[c])

    for c in range(3):
        for i in range(2):
            load(c, i).start()
    for c in range(3):
        for i in range(2):
            load(c, i).wait()
        left[c] = left[c] + right[c]
        store(c).start()
    for c in range(3):
        store(c).wait()


def local(ranks, planes, velocity, row_counts, y_metric, y_curvature):
    length = velocity.shape[3]
    live_total = y_metric.shape[0]
    z_cols, s_cols = length // planes, length // ranks
    far = pl.BlockSpec(memory_space=pltpu.HBM)
    whole = (3, 2, 8, length)
    line, plane = line_table().astype(np.float32), plane_table(planes).astype(np.float32)
    dma = pltpu.SemaphoreType.DMA
    f32, bf16 = jnp.float32, jnp.bfloat16
    parts = pl.pallas_call(
        functools.partial(kernel, ranks, planes, live_total, length),
        out_shape=[jax.ShapeDtypeStruct(whole, f32)] * 2,
        in_specs=[far] * 6,
        out_specs=[far] * 2,
        scratch_shapes=[
            pltpu.VMEM(whole, f32),
            pltpu.VMEM(whole, f32),
            pltpu.SMEM(row_counts.shape, jnp.int32),
            pltpu.SMEM(y_metric.shape, f32),
            pltpu.SMEM(y_curvature.shape, f32),
            pltpu.VMEM(line.shape, f32),
            pltpu.VMEM(plane.shape, f32),
            pltpu.VMEM(line.shape, bf16),
            pltpu.VMEM(line.shape, bf16),
            pltpu.VMEM(plane.shape, bf16),
            pltpu.VMEM(plane.shape, bf16),
            pltpu.VMEM((ranks * STATES, ranks * STATES), f32),
            pltpu.VMEM((48, length + LANES), bf16),
            pltpu.VMEM((48, length + LANES), bf16),
            pltpu.VMEM((2, planes, 3, 8, z_cols), f32),
            pltpu.VMEM((2, planes, 3, 8, z_cols), f32),
            pltpu.VMEM((3, STATES, length), f32),
            pltpu.VMEM((ranks, 3, STATES, s_cols), f32),
            pltpu.VMEM((ranks, 3, STATES, s_cols), f32),
            pltpu.VMEM((3, STATES, length), f32),
            pltpu.VMEM((16, STATES, LANES), f32),
            pltpu.VMEM((22, 2, 2, 8, LANES), f32),
            dma((9,)),
            dma((2, planes)),
            dma((2, planes)),
            dma((2, planes)),
            dma((2, planes)),
            dma((ranks,)),
            dma((ranks,)),
            dma((ranks,)),
            dma((ranks,)),
        ],
        compiler_params=pltpu.CompilerParams(
            collective_id=0, has_side_effects=True, vmem_limit_bytes=63 * 1024 * 1024
        ),
        cost_estimate=pl.CostEstimate(flops=10**9, bytes_accessed=2 * 10**6, transcendentals=10**5),
    )(velocity.reshape(whole), row_counts, y_metric, y_curvature, jnp.asarray(line), jnp.asarray(plane))
    result = pl.pallas_call(
        add_kernel,
        out_shape=jax.ShapeDtypeStruct(whole, f32),
        in_specs=[far] * 2,
        out_specs=far,
        scratch_shapes=[pltpu.VMEM(whole, f32), pltpu.VMEM(whole, f32), dma((3, 2)), dma((3,))],
        compiler_params=pltpu.CompilerParams(vmem_limit_bytes=63 * 1024 * 1024),
        cost_estimate=pl.CostEstimate(flops=2 * 10**5, bytes_accessed=2 * 10**6, transcendentals=0),
    )(*parts)
    return result.reshape(velocity.shape)


def solution(mesh):
    return jax.shard_map(
        functools.partial(local, mesh.shape["row"], mesh.shape["span"]),
        mesh=mesh,
        in_specs=(P(None, "span", "row", None), P(), P(), P()),
        out_specs=P(None, "span", "row", None),
        check_vma=False,
    )
```

```python
import functools
import math

import jax
import jax.numpy as jnp
import numpy as np
from jax import lax
from jax.experimental import pallas as pl
from jax.experimental.pallas import tpu as pltpu
from jax.sharding import PartitionSpec as P

MESH = pl.DeviceIdType.MESH
viscosity = 0.2
LANES = 128
STATES = 8


def scheme(alpha, first):
    root = math.sqrt(1.0 - 4.0 * alpha * alpha)
    decay = (1.0 - root) / (2.0 * alpha)

    def res(s):
        return (-decay) ** abs(s) / root

    def tap(s):
        if first:
            return 0.5 * 14.0 / 9.0 * (res(s - 1) - res(s + 1)) + 0.25 / 9.0 * (res(s - 2) - res(s + 2))
        return (
            12.0 / 11.0 * (res(s - 1) - 2.0 * res(s) + res(s + 1))
            + 0.25 * 3.0 / 11.0 * (res(s - 2) - 2.0 * res(s) + res(s + 2))
        )

    amp = tap(2) / decay**2
    return dict(tap=tap, log=math.log(decay), amp=amp, near=tap(1) + amp * decay, centre=tap(0))


FIRST = scheme(1.0 / 3.0, True)
SECOND = scheme(2.0 / 11.0, False)


def line_table():
    table = np.zeros((2 * LANES, 2 * LANES))
    for p in range(2 * LANES):
        for q in range(LANES):
            shift = p - LANES // 2 - q
            table[p, q] = FIRST["tap"](shift)
            table[p, LANES + q] = viscosity * SECOND["tap"](shift)
    return table


def plane_table(count):
    table = np.zeros((2, count, 8, count, 8))
    for m in range(count):
        for n in range(count):
            for turn in range(-40, 41):
                shift = n - m + turn * count
                for row in range(8):
                    table[0, m, row, n, row] += FIRST["tap"](shift)
                    table[1, m, row, n, row] += viscosity * SECOND["tap"](shift)
    return table.reshape(16 * count, 8 * count)


def split(values):
    high = values.astype(jnp.bfloat16)
    return high, (values - high.astype(jnp.float32)).astype(jnp.bfloat16)


def product(left, right):
    dot = functools.partial(jnp.dot, preferred_element_type=jnp.float32)
    return dot(left[0], right[0]) + (dot(left[0], right[1]) + dot(left[1], right[0]))


def power(log, steps):
    size = jnp.exp(steps.astype(jnp.float32) * log)
    return jnp.where((steps & 1) == 0, size, -size)


def iota(shape, axis):
    return lax.broadcasted_iota(jnp.int32, shape, axis)


def over(count, me, act):
    half = count // 2

    def at(step):
        other = me + step
        act(jnp.where(other >= count, other - count, other), step)

    at(half)

    @pl.loop(0, half - 1)
    def _(index):
        at(half - 1 - index)
        at(half + 1 + index)


def kernel(
    ranks, planes, live_total, length,
    v_far, counts_far, metric_far, curvature_far, line_far, plane_far,
    out_far, z_back,
    out, v, counts, metric, curvature, line, plane, line_high, line_low, plane_high, plane_low, matrix,
    pad_high, pad_low, z_in, z_out, s_out, s_in, s_mid, s_back, s_weight, y_weight,
    local_sem, z_send, z_recv, zb_send, zb_recv, s_send, s_recv, sb_send, sb_recv,
):
    my_row, my_plane = lax.axis_index("row"), lax.axis_index("span")
    z_cols, s_cols = length // planes, length // ranks

    def lanes(start, size=LANES):
        return pl.ds(pl.multiple_of(start, LANES), size)

    def forth(half, source, target, step):
        return pltpu.make_async_remote_copy(
            src_ref=v_far.at[:, half, :, lanes(target * z_cols, z_cols)],
            dst_ref=z_in.at[half, source],
            send_sem=z_send.at[half, step],
            recv_sem=z_recv.at[half, step],
            device_id=(my_row, target),
            device_id_type=MESH,
        )

    def back(half, source, target, step):
        return pltpu.make_async_remote_copy(
            src_ref=z_out.at[half, target],
            dst_ref=z_back.at[:, half, :, lanes(source * z_cols, z_cols)],
            send_sem=zb_send.at[half, step],
            recv_sem=zb_recv.at[half, step],
            device_id=(my_row, target),
            device_id_type=MESH,
        )

    def state_forth(source, target, step):
        return pltpu.make_async_remote_copy(
            src_ref=s_out.at[:, :, lanes(target * s_cols, s_cols)],
            dst_ref=s_in.at[source],
            send_sem=s_send.at[step],
            recv_sem=s_recv.at[step],
            device_id=(target, my_plane),
            device_id_type=MESH,
        )

    def state_back(source, target, step):
        return pltpu.make_async_remote_copy(
            src_ref=s_mid.at[target],
            dst_ref=s_back.at[:, :, lanes(source * s_cols, s_cols)],
            send_sem=sb_send.at[step],
            recv_sem=sb_recv.at[step],
            device_id=(target, my_plane),
            device_id_type=MESH,
        )

    def over_planes(act):
        over(planes, my_plane, act)

    def over_ranks(act):
        over(ranks, my_row, act)

    barrier = pltpu.get_barrier_semaphore()
    over_planes(lambda p, _: pl.semaphore_signal(barrier, 1, device_id=(my_row, p), device_id_type=MESH))
    over_ranks(lambda p, _: pl.semaphore_signal(barrier, 1, device_id=(p, my_plane), device_id_type=MESH))
    pairs = [(counts_far, counts), (v_far, v), (metric_far, metric), (curvature_far, curvature)]
    pairs += [(line_far, line), (plane_far, plane)]
    copies = [pltpu.make_async_copy(*pair, local_sem.at[i]) for i, pair in enumerate(pairs)]
    for copy in copies:
        copy.start()

    copies[0].wait()
    count = counts[my_row]
    kind = iota((STATES, LANES), 0)
    decay_log = jnp.where(kind % 2 == 0, FIRST["log"], SECOND["log"])
    for k in range(16):
        steps = jnp.where(kind < 2, jnp.maximum(count - 1 - k, 0), k)
        weight = jnp.where(kind < 4, power(decay_log, steps), 0.0)
        weight = jnp.where((kind == 4) & (k == 0), 1.0, weight)
        weight = jnp.where((kind == 5) & (count - 1 == k), 1.0, weight)
        s_weight[k] = jnp.where(k < count, weight, 0.0)

    pl.semaphore_wait(barrier, planes + ranks - 2)
    for half in range(2):
        over_planes(lambda p, step, half=half: forth(half, my_plane, p, step).start())
    copies[1].wait()

    @pl.loop(0, length // LANES, unroll=2)
    def _(tile):
        at = lanes(tile * LANES)
        totals = [jnp.zeros((STATES, LANES), jnp.float32)] * 3
        for k in range(16):
            weight = s_weight[k]
            totals = [totals[c] + weight * v[c, k // 8, pl.ds(k % 8, 1), at] for c in range(3)]
        for c in range(3):
            s_out[c, :, at] = totals[c]

    over_ranks(lambda p, step: state_forth(my_row, p, step).start())
    s_in[my_row] = s_out[:, :, lanes(my_row * s_cols, s_cols)]
    for half in range(2):
        z_in[half, my_plane] = v[:, half, :, lanes(my_plane * z_cols, z_cols)]

    for copy in copies[2:]:
        copy.wait()
    line_high[...], line_low[...] = split(line[...])
    plane_high[...], plane_low[...] = split(plane[...])

    for c in range(3):
        turned = pltpu.roll(v[c].reshape(16, length), LANES // 2, 1)
        high, low = split(turned)
        rows = pl.ds(16 * c, 16)
        pad_high[rows, pl.ds(0, length)] = high
        pad_low[rows, pl.ds(0, length)] = low
        pad_high[rows, pl.ds(length, LANES)] = high[:, :LANES]
        pad_low[rows, pl.ds(length, LANES)] = low[:, :LANES]

    group = 8

    def along_x(step):
        def windows(ref):
            return jnp.concatenate(
                [ref[:, lanes((step * group + i) * LANES, 2 * LANES)] for i in range(group)], axis=0
            )

        both = product((windows(pad_high), windows(pad_low)), (line_high[...], line_low[...]))
        for i in range(group):
            at = lanes((step * group + i) * LANES)
            wind = v[0, :, :, at].reshape(16, LANES)
            for c in range(3):
                rows = slice(48 * i + 16 * c, 48 * i + 16 * c + 16)
                part = both[rows, LANES:] - wind * both[rows, :LANES]
                out[c, :, :, at] = part.reshape(2, 8, LANES)

    def keep(half):
        own = z_back.at[:, half, :, lanes(my_plane * z_cols, z_cols)]
        return pltpu.make_async_copy(z_out.at[half, my_plane], own, local_sem.at[7 + half])

    def along_z(half):
        over_planes(lambda p, step: forth(half, p, my_plane, planes - step).wait_recv())
        live = iota((planes, 8, LANES), 1) + 8 * half < count
        for part in range(z_cols // LANES):
            cut = slice(part * LANES, (part + 1) * LANES)
            held = [z_in[half, :, c, :, cut].reshape(8 * planes, LANES) for c in range(3)]
            both = product((plane_high[...], plane_low[...]), split(jnp.concatenate(held, axis=1)))
            for c in range(3):
                at = slice(c * LANES, (c + 1) * LANES)
                term = both[8 * planes :, at] - held[2] * both[: 8 * planes, at]
                z_out[half, :, c, :, cut] = jnp.where(live, term.reshape(planes, 8, LANES), 0.0)
        over_planes(lambda p, step: back(half, my_plane, p, step).start())
        keep(half).start()

    pl.loop(0, length // (LANES * group))(along_x)

    size = ranks * STATES
    col_rank, col_kind = iota((8, size), 1) // STATES, iota((8, size), 1) % STATES
    row_kind = iota((8, size), 0)
    row_log = jnp.where(row_kind % 2 == 0, FIRST["log"], SECOND["log"])
    col_start = col_count = jnp.zeros((8, size), jnp.int32)
    start = jnp.int32(0)
    for rank in range(ranks):
        col_start = col_start + jnp.where(rank < col_rank, counts[rank], 0)
        col_count = jnp.where(rank == col_rank, counts[rank], col_count)
        start = start + jnp.where(rank < my_row, counts[rank], 0)

    def rank_rows(rank, row_start):
        row_count = counts[rank]
        ahead = row_start - col_start - col_count
        ahead = jnp.where(ahead < 0, ahead + live_total, ahead)
        behind = col_start - row_start - row_count
        behind = jnp.where(behind < 0, behind + live_total, behind)
        same = power(row_log, jnp.where(row_kind < 2, ahead, behind))
        rows = jnp.where((row_kind == col_kind) & (row_kind < 4), same, 0.0)
        rows = jnp.where((row_kind == 4) & (col_kind == 5) & (ahead == 0), 1.0, rows)
        rows = jnp.where((row_kind == 5) & (col_kind == 4) & (behind == 0), 1.0, rows)
        matrix[pl.ds(pl.multiple_of(rank * STATES, STATES), STATES), :] = rows
        return row_start + row_count

    lax.fori_loop(0, ranks, rank_rows, jnp.int32(0), unroll=4)

    def over_y():
        over_ranks(lambda p, step: state_forth(p, my_row, ranks - step).wait_recv())
        held = [s_in[:, c].reshape(size, s_cols) for c in range(3)]
        both = product(split(matrix[...]), split(jnp.concatenate(held, axis=1)))
        for c in range(3):
            s_mid[:, c] = both[:, c * s_cols : (c + 1) * s_cols].reshape(ranks, STATES, s_cols)
        over_ranks(lambda p, step: state_back(my_row, p, step).start())
        s_back[:, :, lanes(my_row * s_cols, s_cols)] = s_mid[my_row]

    for half in range(2):
        slot = iota((8, LANES), 0) + 8 * half
        stretch = jnp.zeros((8, LANES), jnp.float32)
        bend = jnp.zeros((8, LANES), jnp.float32)
        for k in range(8 * half, 8 * half + 8):
            grid_row = jnp.minimum(start + k, live_total - 1)
            stretch = jnp.where(slot == k, metric[grid_row], stretch)
            bend = jnp.where(slot == k, curvature[grid_row], bend)
        live = slot < count
        tail = jnp.maximum(count - slot, 0)
        for term in range(16 + 6):
            if term < 16:
                away = jnp.abs(term - slot)
                one = FIRST["amp"] * power(FIRST["log"], away) + jnp.where(away == 1, FIRST["near"], 0.0)
                one = jnp.where(away == 0, 0.0, jnp.where(term > slot, one, -one))
                two = SECOND["amp"] * power(SECOND["log"], away) + jnp.where(away == 1, SECOND["near"], 0.0)
                two = jnp.where(away == 0, SECOND["centre"], two)
                used = live & (term < count)
            else:
                one = two = jnp.zeros((8, LANES), jnp.float32)
                used = live
                if term == 16:
                    one = -FIRST["amp"] * power(FIRST["log"], slot + 1)
                if term == 17:
                    two = SECOND["amp"] * power(SECOND["log"], slot + 1)
                if term == 18:
                    one = FIRST["amp"] * power(FIRST["log"], tail)
                if term == 19:
                    two = SECOND["amp"] * power(SECOND["log"], tail)
                if term == 20:
                    one = jnp.where(slot == 0, -FIRST["near"], 0.0)
                    two = jnp.where(slot == 0, SECOND["near"], 0.0)
                if term == 21:
                    one = jnp.where(tail == 1, FIRST["near"], 0.0)
                    two = jnp.where(tail == 1, SECOND["near"], 0.0)
            y_weight[term, half, 0] = jnp.where(used, stretch * one, 0.0)
            y_weight[term, half, 1] = jnp.where(
                used, viscosity * (stretch * stretch * two + bend * one), 0.0
            )

    along_z(0)
    along_z(1)
    over_y()
    for half in range(2):
        over_planes(lambda p, step, half=half: forth(half, my_plane, p, step).wait_send())
    over_ranks(lambda p, step: state_forth(my_row, p, step).wait_send())
    over_ranks(lambda p, step: state_back(p, my_row, ranks - step).wait_recv())

    def along_y(tile):
        at = lanes(tile * LANES)
        sums = [[[jnp.zeros((8, LANES), jnp.float32)] * 2 for _ in range(2)] for _ in range(3)]
        for term in range(16 + 6):
            for c in range(3):
                if term < 16:
                    row = v[c, term // 8, pl.ds(term % 8, 1), at]
                else:
                    row = s_back[c, pl.ds(term - 16, 1), at]
                for half in range(2):
                    sums[c][half] = [sums[c][half][i] + y_weight[term, half, i] * row for i in range(2)]
        for half in range(2):
            wind = v[1, half, :, at]
            live = iota((8, LANES), 0) + 8 * half < count
            for c in range(3):
                term = out[c, half, :, at] + sums[c][half][1] - wind * sums[c][half][0]
                out[c, half, :, at] = jnp.where(live, term, 0.0)

    pl.loop(0, length // LANES)(along_y)
    leave = pltpu.make_async_copy(out, out_far, local_sem.at[6])
    leave.start()
    over_ranks(lambda p, step: state_back(my_row, p, step).wait_send())
    for half in range(2):
        over_planes(lambda p, step, half=half: back(half, my_plane, p, step).wait_send())
    for half in range(2):
        over_planes(lambda p, step, half=half: back(half, p, my_plane, planes - step).wait_recv())
        keep(half).wait()
    leave.wait()


def add_kernel(left_far, right_far, out_far, left, right, load_sem, store_sem):
    def load(c, i):
        return pltpu.make_async_copy((left_far, right_far)[i].at[c], (left, right)[i].at[c], load_sem.at[c, i])

    def store(c):
        return pltpu.make_async_copy(left.at[c], out_far.at[c], store_sem.at[c])

    for c in range(3):
        for i in range(2):
            load(c, i).start()
    for c in range(3):
        for i in range(2):
            load(c, i).wait()
        left[c] = left[c] + right[c]
        store(c).start()
    for c in range(3):
        store(c).wait()


def local(ranks, planes, velocity, row_counts, y_metric, y_curvature):
    length = velocity.shape[3]
    live_total = y_metric.shape[0]
    z_cols, s_cols = length // planes, length // ranks
    far = pl.BlockSpec(memory_space=pltpu.HBM)
    whole = (3, 2, 8, length)
    line, plane = line_table().astype(np.float32), plane_table(planes).astype(np.float32)
    dma = pltpu.SemaphoreType.DMA
    f32, bf16 = jnp.float32, jnp.bfloat16
    parts = pl.pallas_call(
        functools.partial(kernel, ranks, planes, live_total, length),
        out_shape=[jax.ShapeDtypeStruct(whole, f32)] * 2,
        in_specs=[far] * 6,
        out_specs=[far] * 2,
        scratch_shapes=[
            pltpu.VMEM(whole, f32),
            pltpu.VMEM(whole, f32),
            pltpu.SMEM(row_counts.shape, jnp.int32),
            pltpu.SMEM(y_metric.shape, f32),
            pltpu.SMEM(y_curvature.shape, f32),
            pltpu.VMEM(line.shape, f32),
            pltpu.VMEM(plane.shape, f32),
            pltpu.VMEM(line.shape, bf16),
            pltpu.VMEM(line.shape, bf16),
            pltpu.VMEM(plane.shape, bf16),
            pltpu.VMEM(plane.shape, bf16),
            pltpu.VMEM((ranks * STATES, ranks * STATES), f32),
            pltpu.VMEM((48, length + LANES), bf16),
            pltpu.VMEM((48, length + LANES), bf16),
            pltpu.VMEM((2, planes, 3, 8, z_cols), f32),
            pltpu.VMEM((2, planes, 3, 8, z_cols), f32),
            pltpu.VMEM((3, STATES, length), f32),
            pltpu.VMEM((ranks, 3, STATES, s_cols), f32),
            pltpu.VMEM((ranks, 3, STATES, s_cols), f32),
            pltpu.VMEM((3, STATES, length), f32),
            pltpu.VMEM((16, STATES, LANES), f32),
            pltpu.VMEM((22, 2, 2, 8, LANES), f32),
            dma((9,)),
            dma((2, planes)),
            dma((2, planes)),
            dma((2, planes)),
            dma((2, planes)),
            dma((ranks,)),
            dma((ranks,)),
            dma((ranks,)),
            dma((ranks,)),
        ],
        compiler_params=pltpu.CompilerParams(
            collective_id=0, has_side_effects=True, vmem_limit_bytes=63 * 1024 * 1024
        ),
        cost_estimate=pl.CostEstimate(flops=10**9, bytes_accessed=2 * 10**6, transcendentals=10**5),
    )(velocity.reshape(whole), row_counts, y_metric, y_curvature, jnp.asarray(line), jnp.asarray(plane))
    result = pl.pallas_call(
        add_kernel,
        out_shape=jax.ShapeDtypeStruct(whole, f32),
        in_specs=[far] * 2,
        out_specs=far,
        scratch_shapes=[pltpu.VMEM(whole, f32), pltpu.VMEM(whole, f32), dma((3, 2)), dma((3,))],
        compiler_params=pltpu.CompilerParams(vmem_limit_bytes=63 * 1024 * 1024),
        cost_estimate=pl.CostEstimate(flops=2 * 10**5, bytes_accessed=2 * 10**6, transcendentals=0),
    )(*parts)
    return result.reshape(velocity.shape)


def solution(mesh):
    return jax.shard_map(
        functools.partial(local, mesh.shape["row"], mesh.shape["span"]),
        mesh=mesh,
        in_specs=(P(None, "span", "row", None), P(), P(), P()),
        out_specs=P(None, "span", "row", None),
        check_vma=False,
    )
```

```python
import functools
import math

import jax
import jax.numpy as jnp
import numpy as np
from jax import lax
from jax.experimental import pallas as pl
from jax.experimental.pallas import tpu as pltpu
from jax.sharding import PartitionSpec as P

MESH = pl.DeviceIdType.MESH
viscosity = 0.2
LANES = 128
STATES = 8


def scheme(alpha, first):
    root = math.sqrt(1.0 - 4.0 * alpha * alpha)
    decay = (1.0 - root) / (2.0 * alpha)

    def res(s):
        return (-decay) ** abs(s) / root

    def tap(s):
        if first:
            return 0.5 * 14.0 / 9.0 * (res(s - 1) - res(s + 1)) + 0.25 / 9.0 * (res(s - 2) - res(s + 2))
        return (
            12.0 / 11.0 * (res(s - 1) - 2.0 * res(s) + res(s + 1))
            + 0.25 * 3.0 / 11.0 * (res(s - 2) - 2.0 * res(s) + res(s + 2))
        )

    amp = tap(2) / decay**2
    return dict(tap=tap, log=math.log(decay), amp=amp, near=tap(1) + amp * decay, centre=tap(0))


FIRST = scheme(1.0 / 3.0, True)
SECOND = scheme(2.0 / 11.0, False)


def line_table():
    table = np.zeros((2 * LANES, 2 * LANES))
    for p in range(2 * LANES):
        for q in range(LANES):
            shift = p - LANES // 2 - q
            table[p, q] = FIRST["tap"](shift)
            table[p, LANES + q] = viscosity * SECOND["tap"](shift)
    return table


def plane_table(count):
    table = np.zeros((2, count, 8, count, 8))
    for m in range(count):
        for n in range(count):
            for turn in range(-40, 41):
                shift = n - m + turn * count
                for row in range(8):
                    table[0, m, row, n, row] += FIRST["tap"](shift)
                    table[1, m, row, n, row] += viscosity * SECOND["tap"](shift)
    return table.reshape(16 * count, 8 * count)


def split(values):
    high = values.astype(jnp.bfloat16)
    return high, (values - high.astype(jnp.float32)).astype(jnp.bfloat16)


def product(left, right):
    dot = functools.partial(jnp.dot, preferred_element_type=jnp.float32)
    return dot(left[0], right[0]) + (dot(left[0], right[1]) + dot(left[1], right[0]))


def power(log, steps):
    size = jnp.exp(steps.astype(jnp.float32) * log)
    return jnp.where((steps & 1) == 0, size, -size)


def iota(shape, axis):
    return lax.broadcasted_iota(jnp.int32, shape, axis)


def over(count, me, act):
    half = count // 2

    def at(step):
        other = me + step
        act(jnp.where(other >= count, other - count, other), step)

    at(half)

    @pl.loop(0, half - 1)
    def _(index):
        at(half - 1 - index)
        at(half + 1 + index)


def kernel(
    ranks, planes, live_total, length,
    v_far, counts_far, metric_far, curvature_far, line_far, plane_far,
    out_far, z_back,
    out, v, counts, metric, curvature, line, plane, line_high, line_low, plane_high, plane_low, matrix,
    pad_high, pad_low, z_in, z_out, s_out, s_in, s_mid, s_back, s_weight, y_weight,
    local_sem, z_send, z_recv, zb_send, zb_recv, s_send, s_recv, sb_send, sb_recv,
):
    my_row, my_plane = lax.axis_index("row"), lax.axis_index("span")
    z_cols, s_cols = length // planes, length // ranks

    def lanes(start, size=LANES):
        return pl.ds(pl.multiple_of(start, LANES), size)

    def forth(half, source, target, step):
        return pltpu.make_async_remote_copy(
            src_ref=v_far.at[:, half, :, lanes(target * z_cols, z_cols)],
            dst_ref=z_in.at[half, source],
            send_sem=z_send.at[half, step],
            recv_sem=z_recv.at[half, step],
            device_id=(my_row, target),
            device_id_type=MESH,
        )

    def back(half, source, target, step):
        return pltpu.make_async_remote_copy(
            src_ref=z_out.at[half, target],
            dst_ref=z_back.at[:, half, :, lanes(source * z_cols, z_cols)],
            send_sem=zb_send.at[half, step],
            recv_sem=zb_recv.at[half, step],
            device_id=(my_row, target),
            device_id_type=MESH,
        )

    def state_forth(source, target, step):
        return pltpu.make_async_remote_copy(
            src_ref=s_out.at[:, :, lanes(target * s_cols, s_cols)],
            dst_ref=s_in.at[source],
            send_sem=s_send.at[step],
            recv_sem=s_recv.at[step],
            device_id=(target, my_plane),
            device_id_type=MESH,
        )

    def state_back(source, target, step):
        return pltpu.make_async_remote_copy(
            src_ref=s_mid.at[target],
            dst_ref=s_back.at[:, :, lanes(source * s_cols, s_cols)],
            send_sem=sb_send.at[step],
            recv_sem=sb_recv.at[step],
            device_id=(target, my_plane),
            device_id_type=MESH,
        )

    def over_planes(act):
        over(planes, my_plane, act)

    def over_ranks(act):
        over(ranks, my_row, act)

    barrier = pltpu.get_barrier_semaphore()
    over_planes(lambda p, _: pl.semaphore_signal(barrier, 1, device_id=(my_row, p), device_id_type=MESH))
    over_ranks(lambda p, _: pl.semaphore_signal(barrier, 1, device_id=(p, my_plane), device_id_type=MESH))
    pairs = [(counts_far, counts), (v_far, v), (metric_far, metric), (curvature_far, curvature)]
    pairs += [(line_far, line), (plane_far, plane)]
    copies = [pltpu.make_async_copy(*pair, local_sem.at[i]) for i, pair in enumerate(pairs)]
    for copy in copies:
        copy.start()

    copies[0].wait()
    count = counts[my_row]
    kind = iota((STATES, LANES), 0)
    decay_log = jnp.where(kind % 2 == 0, FIRST["log"], SECOND["log"])
    for k in range(16):
        steps = jnp.where(kind < 2, jnp.maximum(count - 1 - k, 0), k)
        weight = jnp.where(kind < 4, power(decay_log, steps), 0.0)
        weight = jnp.where((kind == 4) & (k == 0), 1.0, weight)
        weight = jnp.where((kind == 5) & (count - 1 == k), 1.0, weight)
        s_weight[k] = jnp.where(k < count, weight, 0.0)

    pl.semaphore_wait(barrier, planes + ranks - 2)
    over_planes(lambda p, step: forth(0, my_plane, p, step).start())
    copies[1].wait()

    @pl.loop(0, length // LANES, unroll=2)
    def _(tile):
        at = lanes(tile * LANES)
        totals = [jnp.zeros((STATES, LANES), jnp.float32)] * 3
        for k in range(16):
            weight = s_weight[k]
            totals = [totals[c] + weight * v[c, k // 8, pl.ds(k % 8, 1), at] for c in range(3)]
        for c in range(3):
            s_out[c, :, at] = totals[c]

    over_ranks(lambda p, step: state_forth(my_row, p, step).start())
    s_in[my_row] = s_out[:, :, lanes(my_row * s_cols, s_cols)]
    for half in range(2):
        z_in[half, my_plane] = v[:, half, :, lanes(my_plane * z_cols, z_cols)]

    for copy in copies[2:]:
        copy.wait()
    line_high[...], line_low[...] = split(line[...])
    plane_high[...], plane_low[...] = split(plane[...])

    for c in range(3):
        turned = pltpu.roll(v[c].reshape(16, length), LANES // 2, 1)
        high, low = split(turned)
        rows = pl.ds(16 * c, 16)
        pad_high[rows, pl.ds(0, length)] = high
        pad_low[rows, pl.ds(0, length)] = low
        pad_high[rows, pl.ds(length, LANES)] = high[:, :LANES]
        pad_low[rows, pl.ds(length, LANES)] = low[:, :LANES]

    over_planes(lambda p, step: forth(1, my_plane, p, step).start())

    group = 8

    def along_x(step):
        def windows(ref):
            return jnp.concatenate(
                [ref[:, lanes((step * group + i) * LANES, 2 * LANES)] for i in range(group)], axis=0
            )

        both = product((windows(pad_high), windows(pad_low)), (line_high[...], line_low[...]))
        for i in range(group):
            at = lanes((step * group + i) * LANES)
            wind = v[0, :, :, at].reshape(16, LANES)
            for c in range(3):
                rows = slice(48 * i + 16 * c, 48 * i + 16 * c + 16)
                part = both[rows, LANES:] - wind * both[rows, :LANES]
                out[c, :, :, at] = part.reshape(2, 8, LANES)

    def keep(half):
        own = z_back.at[:, half, :, lanes(my_plane * z_cols, z_cols)]
        return pltpu.make_async_copy(z_out.at[half, my_plane], own, local_sem.at[7 + half])

    def along_z(half):
        over_planes(lambda p, step: forth(half, p, my_plane, planes - step).wait_recv())
        live = iota((planes, 8, LANES), 1) + 8 * half < count
        for part in range(z_cols // LANES):
            cut = slice(part * LANES, (part + 1) * LANES)
            held = [z_in[half, :, c, :, cut].reshape(8 * planes, LANES) for c in range(3)]
            both = product((plane_high[...], plane_low[...]), split(jnp.concatenate(held, axis=1)))
            for c in range(3):
                at = slice(c * LANES, (c + 1) * LANES)
                term = both[8 * planes :, at] - held[2] * both[: 8 * planes, at]
                z_out[half, :, c, :, cut] = jnp.where(live, term.reshape(planes, 8, LANES), 0.0)
        over_planes(lambda p, step: back(half, my_plane, p, step).start())
        keep(half).start()

    pl.loop(0, length // (LANES * group))(along_x)

    size = ranks * STATES
    col_rank, col_kind = iota((8, size), 1) // STATES, iota((8, size), 1) % STATES
    row_kind = iota((8, size), 0)
    row_log = jnp.where(row_kind % 2 == 0, FIRST["log"], SECOND["log"])
    col_start = col_count = jnp.zeros((8, size), jnp.int32)
    start = jnp.int32(0)
    for rank in range(ranks):
        col_start = col_start + jnp.where(rank < col_rank, counts[rank], 0)
        col_count = jnp.where(rank == col_rank, counts[rank], col_count)
        start = start + jnp.where(rank < my_row, counts[rank], 0)

    def rank_rows(rank, row_start):
        row_count = counts[rank]
        ahead = row_start - col_start - col_count
        ahead = jnp.where(ahead < 0, ahead + live_total, ahead)
        behind = col_start - row_start - row_count
        behind = jnp.where(behind < 0, behind + live_total, behind)
        same = power(row_log, jnp.where(row_kind < 2, ahead, behind))
        rows = jnp.where((row_kind == col_kind) & (row_kind < 4), same, 0.0)
        rows = jnp.where((row_kind == 4) & (col_kind == 5) & (ahead == 0), 1.0, rows)
        rows = jnp.where((row_kind == 5) & (col_kind == 4) & (behind == 0), 1.0, rows)
        matrix[pl.ds(pl.multiple_of(rank * STATES, STATES), STATES), :] = rows
        return row_start + row_count

    lax.fori_loop(0, ranks, rank_rows, jnp.int32(0), unroll=4)

    def over_y():
        over_ranks(lambda p, step: state_forth(p, my_row, ranks - step).wait_recv())
        held = [s_in[:, c].reshape(size, s_cols) for c in range(3)]
        both = product(split(matrix[...]), split(jnp.concatenate(held, axis=1)))
        for c in range(3):
            s_mid[:, c] = both[:, c * s_cols : (c + 1) * s_cols].reshape(ranks, STATES, s_cols)
        over_ranks(lambda p, step: state_back(my_row, p, step).start())
        s_back[:, :, lanes(my_row * s_cols, s_cols)] = s_mid[my_row]

    for half in range(2):
        slot = iota((8, LANES), 0) + 8 * half
        stretch = jnp.zeros((8, LANES), jnp.float32)
        bend = jnp.zeros((8, LANES), jnp.float32)
        for k in range(8 * half, 8 * half + 8):
            grid_row = jnp.minimum(start + k, live_total - 1)
            stretch = jnp.where(slot == k, metric[grid_row], stretch)
            bend = jnp.where(slot == k, curvature[grid_row], bend)
        live = slot < count
        tail = jnp.maximum(count - slot, 0)
        for term in range(16 + 6):
            if term < 16:
                away = jnp.abs(term - slot)
                one = FIRST["amp"] * power(FIRST["log"], away) + jnp.where(away == 1, FIRST["near"], 0.0)
                one = jnp.where(away == 0, 0.0, jnp.where(term > slot, one, -one))
                two = SECOND["amp"] * power(SECOND["log"], away) + jnp.where(away == 1, SECOND["near"], 0.0)
                two = jnp.where(away == 0, SECOND["centre"], two)
                used = live & (term < count)
            else:
                one = two = jnp.zeros((8, LANES), jnp.float32)
                used = live
                if term == 16:
                    one = -FIRST["amp"] * power(FIRST["log"], slot + 1)
                if term == 17:
                    two = SECOND["amp"] * power(SECOND["log"], slot + 1)
                if term == 18:
                    one = FIRST["amp"] * power(FIRST["log"], tail)
                if term == 19:
                    two = SECOND["amp"] * power(SECOND["log"], tail)
                if term == 20:
                    one = jnp.where(slot == 0, -FIRST["near"], 0.0)
                    two = jnp.where(slot == 0, SECOND["near"], 0.0)
                if term == 21:
                    one = jnp.where(tail == 1, FIRST["near"], 0.0)
                    two = jnp.where(tail == 1, SECOND["near"], 0.0)
            y_weight[term, half, 0] = jnp.where(used, stretch * one, 0.0)
            y_weight[term, half, 1] = jnp.where(
                used, viscosity * (stretch * stretch * two + bend * one), 0.0
            )

    along_z(0)
    along_z(1)
    over_y()
    for half in range(2):
        over_planes(lambda p, step, half=half: forth(half, my_plane, p, step).wait_send())
    over_ranks(lambda p, step: state_forth(my_row, p, step).wait_send())
    over_ranks(lambda p, step: state_back(p, my_row, ranks - step).wait_recv())

    def along_y(tile):
        at = lanes(tile * LANES)
        sums = [[[jnp.zeros((8, LANES), jnp.float32)] * 2 for _ in range(2)] for _ in range(3)]
        for term in range(16 + 6):
            for c in range(3):
                if term < 16:
                    row = v[c, term // 8, pl.ds(term % 8, 1), at]
                else:
                    row = s_back[c, pl.ds(term - 16, 1), at]
                for half in range(2):
                    sums[c][half] = [sums[c][half][i] + y_weight[term, half, i] * row for i in range(2)]
        for half in range(2):
            wind = v[1, half, :, at]
            live = iota((8, LANES), 0) + 8 * half < count
            for c in range(3):
                term = out[c, half, :, at] + sums[c][half][1] - wind * sums[c][half][0]
                out[c, half, :, at] = jnp.where(live, term, 0.0)

    pl.loop(0, length // LANES)(along_y)
    leave = pltpu.make_async_copy(out, out_far, local_sem.at[6])
    leave.start()
    over_ranks(lambda p, step: state_back(my_row, p, step).wait_send())
    for half in range(2):
        over_planes(lambda p, step, half=half: back(half, my_plane, p, step).wait_send())
    for half in range(2):
        over_planes(lambda p, step, half=half: back(half, p, my_plane, planes - step).wait_recv())
        keep(half).wait()
    leave.wait()


def add_kernel(left_far, right_far, out_far, left, right, load_sem, store_sem):
    parts = [(c, half) for c in range(3) for half in range(2)]

    def load(at, i):
        return pltpu.make_async_copy((left_far, right_far)[i].at[at], (left, right)[i].at[at], load_sem.at[*at, i])

    def store(at):
        return pltpu.make_async_copy(left.at[at], out_far.at[at], store_sem.at[*at])

    for at in parts:
        for i in range(2):
            load(at, i).start()
    for at in parts:
        for i in range(2):
            load(at, i).wait()
        left[at] = left[at] + right[at]
        store(at).start()
    for at in parts:
        store(at).wait()


def local(ranks, planes, velocity, row_counts, y_metric, y_curvature):
    length = velocity.shape[3]
    live_total = y_metric.shape[0]
    z_cols, s_cols = length // planes, length // ranks
    far = pl.BlockSpec(memory_space=pltpu.HBM)
    whole = (3, 2, 8, length)
    line, plane = line_table().astype(np.float32), plane_table(planes).astype(np.float32)
    dma = pltpu.SemaphoreType.DMA
    f32, bf16 = jnp.float32, jnp.bfloat16
    parts = pl.pallas_call(
        functools.partial(kernel, ranks, planes, live_total, length),
        out_shape=[jax.ShapeDtypeStruct(whole, f32)] * 2,
        in_specs=[far] * 6,
        out_specs=[far] * 2,
        scratch_shapes=[
            pltpu.VMEM(whole, f32),
            pltpu.VMEM(whole, f32),
            pltpu.SMEM(row_counts.shape, jnp.int32),
            pltpu.SMEM(y_metric.shape, f32),
            pltpu.SMEM(y_curvature.shape, f32),
            pltpu.VMEM(line.shape, f32),
            pltpu.VMEM(plane.shape, f32),
            pltpu.VMEM(line.shape, bf16),
            pltpu.VMEM(line.shape, bf16),
            pltpu.VMEM(plane.shape, bf16),
            pltpu.VMEM(plane.shape, bf16),
            pltpu.VMEM((ranks * STATES, ranks * STATES), f32),
            pltpu.VMEM((48, length + LANES), bf16),
            pltpu.VMEM((48, length + LANES), bf16),
            pltpu.VMEM((2, planes, 3, 8, z_cols), f32),
            pltpu.VMEM((2, planes, 3, 8, z_cols), f32),
            pltpu.VMEM((3, STATES, length), f32),
            pltpu.VMEM((ranks, 3, STATES, s_cols), f32),
            pltpu.VMEM((ranks, 3, STATES, s_cols), f32),
            pltpu.VMEM((3, STATES, length), f32),
            pltpu.VMEM((16, STATES, LANES), f32),
            pltpu.VMEM((22, 2, 2, 8, LANES), f32),
            dma((9,)),
            dma((2, planes)),
            dma((2, planes)),
            dma((2, planes)),
            dma((2, planes)),
            dma((ranks,)),
            dma((ranks,)),
            dma((ranks,)),
            dma((ranks,)),
        ],
        compiler_params=pltpu.CompilerParams(
            collective_id=0, has_side_effects=True, vmem_limit_bytes=63 * 1024 * 1024
        ),
        cost_estimate=pl.CostEstimate(flops=10**9, bytes_accessed=2 * 10**6, transcendentals=10**5),
    )(velocity.reshape(whole), row_counts, y_metric, y_curvature, jnp.asarray(line), jnp.asarray(plane))
    result = pl.pallas_call(
        add_kernel,
        out_shape=jax.ShapeDtypeStruct(whole, f32),
        in_specs=[far] * 2,
        out_specs=far,
        scratch_shapes=[pltpu.VMEM(whole, f32), pltpu.VMEM(whole, f32), dma((3, 2, 2)), dma((3, 2))],
        compiler_params=pltpu.CompilerParams(vmem_limit_bytes=63 * 1024 * 1024),
        cost_estimate=pl.CostEstimate(flops=2 * 10**5, bytes_accessed=2 * 10**6, transcendentals=0),
    )(*parts)
    return result.reshape(velocity.shape)


def solution(mesh):
    return jax.shard_map(
        functools.partial(local, mesh.shape["row"], mesh.shape["span"]),
        mesh=mesh,
        in_specs=(P(None, "span", "row", None), P(), P(), P()),
        out_specs=P(None, "span", "row", None),
        check_vma=False,
    )
```

```python
import functools
import math

import jax
import jax.numpy as jnp
import numpy as np
from jax import lax
from jax.experimental import pallas as pl
from jax.experimental.pallas import tpu as pltpu
from jax.sharding import PartitionSpec as P

MESH = pl.DeviceIdType.MESH
viscosity = 0.2
LANES = 128
STATES = 8


def scheme(alpha, first):
    root = math.sqrt(1.0 - 4.0 * alpha * alpha)
    decay = (1.0 - root) / (2.0 * alpha)

    def res(s):
        return (-decay) ** abs(s) / root

    def tap(s):
        if first:
            return 0.5 * 14.0 / 9.0 * (res(s - 1) - res(s + 1)) + 0.25 / 9.0 * (res(s - 2) - res(s + 2))
        return (
            12.0 / 11.0 * (res(s - 1) - 2.0 * res(s) + res(s + 1))
            + 0.25 * 3.0 / 11.0 * (res(s - 2) - 2.0 * res(s) + res(s + 2))
        )

    amp = tap(2) / decay**2
    return dict(tap=tap, log=math.log(decay), amp=amp, near=tap(1) + amp * decay, centre=tap(0))


FIRST = scheme(1.0 / 3.0, True)
SECOND = scheme(2.0 / 11.0, False)


def line_table():
    table = np.zeros((2 * LANES, 2 * LANES))
    for p in range(2 * LANES):
        for q in range(LANES):
            shift = p - LANES // 2 - q
            table[p, q] = FIRST["tap"](shift)
            table[p, LANES + q] = viscosity * SECOND["tap"](shift)
    return table


def plane_table(count):
    table = np.zeros((2, count, 8, count, 8))
    for m in range(count):
        for n in range(count):
            for turn in range(-40, 41):
                shift = n - m + turn * count
                for row in range(8):
                    table[0, m, row, n, row] += FIRST["tap"](shift)
                    table[1, m, row, n, row] += viscosity * SECOND["tap"](shift)
    return table.reshape(16 * count, 8 * count)


def split(values):
    high = values.astype(jnp.bfloat16)
    return high, (values - high.astype(jnp.float32)).astype(jnp.bfloat16)


def product(left, right):
    dot = functools.partial(jnp.dot, preferred_element_type=jnp.float32)
    return dot(left[0], right[0]) + (dot(left[0], right[1]) + dot(left[1], right[0]))


def power(log, steps):
    size = jnp.exp(steps.astype(jnp.float32) * log)
    return jnp.where((steps & 1) == 0, size, -size)


def iota(shape, axis):
    return lax.broadcasted_iota(jnp.int32, shape, axis)


def over(count, me, act):
    half = count // 2

    def at(step):
        other = me + step
        act(jnp.where(other >= count, other - count, other), step)

    at(half)

    @pl.loop(0, half - 1)
    def _(index):
        at(half - 1 - index)
        at(half + 1 + index)


def kernel(
    ranks, planes, live_total, length,
    v_far, counts_far, metric_far, curvature_far, line_far, plane_far,
    out_far, z_back,
    out, v, counts, metric, curvature, line, plane, line_high, line_low, plane_high, plane_low, matrix,
    pad_high, pad_low, z_in, z_out, relay, s_out, s_in, s_mid, s_back, s_weight, y_weight,
    local_sem, z_send, z_recv, zb_send, zb_recv, s_send, s_recv, sb_send, sb_recv, relay_sem,
):
    my_row, my_plane = lax.axis_index("row"), lax.axis_index("span")
    z_cols, s_cols = length // planes, length // ranks

    def lanes(start, size=LANES):
        return pl.ds(pl.multiple_of(start, LANES), size)

    def forth(half, source, target, step):
        return pltpu.make_async_remote_copy(
            src_ref=v_far.at[:, half, :, lanes(target * z_cols, z_cols)],
            dst_ref=z_in.at[half, source],
            send_sem=z_send.at[half, step],
            recv_sem=z_recv.at[half, step],
            device_id=(my_row, target),
            device_id_type=MESH,
        )

    def back(half, source, target, step):
        return pltpu.make_async_remote_copy(
            src_ref=z_out.at[half, target],
            dst_ref=z_back.at[:, half, :, lanes(source * z_cols, z_cols)],
            send_sem=zb_send.at[half, step],
            recv_sem=zb_recv.at[half, step],
            device_id=(my_row, target),
            device_id_type=MESH,
        )

    def state_forth(source, target, step):
        return pltpu.make_async_remote_copy(
            src_ref=s_out.at[:, :, lanes(target * s_cols, s_cols)],
            dst_ref=s_in.at[source],
            send_sem=s_send.at[step],
            recv_sem=s_recv.at[step],
            device_id=(target, my_plane),
            device_id_type=MESH,
        )

    def state_back(source, target, step):
        return pltpu.make_async_remote_copy(
            src_ref=s_mid.at[target],
            dst_ref=s_back.at[:, :, lanes(source * s_cols, s_cols)],
            send_sem=sb_send.at[step],
            recv_sem=sb_recv.at[step],
            device_id=(target, my_plane),
            device_id_type=MESH,
        )

    def over_planes(act):
        over(planes, my_plane, act)

    def over_ranks(act):
        over(ranks, my_row, act)

    chips, my_core = planes // 2, my_plane % 2
    reach = chips // 2
    far_steps = [chips, chips + 1 - 2 * my_core]

    def around(step):
        place = my_plane + step
        return jnp.where(place >= planes, place - planes, place)

    relays = [around(reach), around(planes - reach)]
    finals = [around(step) for step in far_steps]
    origins = [around(planes - reach), around(reach)]
    goals = [around(reach), around(planes - reach) + 1 - 2 * my_core]

    def over_near(act):
        def at(step):
            act(around(step), step)

        at(chips - 1 + 2 * my_core)

        @pl.loop(1, chips - 1)
        def _(index):
            at(chips - 1 - index)
            at(chips + 1 + index)

    def relay_first(held, half, way, src):
        return pltpu.make_async_remote_copy(
            src_ref=src,
            dst_ref=relay.at[held, half, way],
            send_sem=relay_sem.at[held, 0, half, way],
            recv_sem=relay_sem.at[held, 1, half, way],
            device_id=(my_row, relays[way]),
            device_id_type=MESH,
        )

    def forth_first(half, way):
        return relay_first(0, half, way, v_far.at[:, half, :, lanes(finals[way] * z_cols, z_cols)])

    def back_first(half, way):
        return relay_first(1, half, way, z_out.at[half, finals[way]])

    def forth_second(half, way):
        return pltpu.make_async_remote_copy(
            src_ref=relay.at[0, half, way],
            dst_ref=z_in.at[half, origins[way]],
            send_sem=relay_sem.at[0, 2, half, way],
            recv_sem=z_recv.at[half, far_steps[way]],
            device_id=(my_row, goals[way]),
            device_id_type=MESH,
        )

    def back_second(half, way):
        return pltpu.make_async_remote_copy(
            src_ref=relay.at[1, half, way],
            dst_ref=z_back.at[:, half, :, lanes(origins[way] * z_cols, z_cols)],
            send_sem=relay_sem.at[1, 2, half, way],
            recv_sem=zb_recv.at[half, far_steps[way]],
            device_id=(my_row, goals[way]),
            device_id_type=MESH,
        )

    def send(first, direct, half):
        for way in range(2):
            first(half, way).start()
        over_near(lambda p, step: direct(half, my_plane, p, step).start())

    def pass_on(first, second, half):
        for way in range(2):
            first(half, way).wait_recv()
            second(half, way).start()

    def sent(first, second, direct, half):
        for way in range(2):
            first(half, way).wait_send()
            second(half, way).wait_send()
        over_near(lambda p, step: direct(half, my_plane, p, step).wait_send())

    barrier = pltpu.get_barrier_semaphore()
    over_planes(lambda p, _: pl.semaphore_signal(barrier, 1, device_id=(my_row, p), device_id_type=MESH))
    over_ranks(lambda p, _: pl.semaphore_signal(barrier, 1, device_id=(p, my_plane), device_id_type=MESH))
    pairs = [(counts_far, counts), (v_far, v), (metric_far, metric), (curvature_far, curvature)]
    pairs += [(line_far, line), (plane_far, plane)]
    copies = [pltpu.make_async_copy(*pair, local_sem.at[i]) for i, pair in enumerate(pairs)]
    for copy in copies:
        copy.start()

    copies[0].wait()
    count = counts[my_row]
    kind = iota((STATES, LANES), 0)
    decay_log = jnp.where(kind % 2 == 0, FIRST["log"], SECOND["log"])
    for k in range(16):
        steps = jnp.where(kind < 2, jnp.maximum(count - 1 - k, 0), k)
        weight = jnp.where(kind < 4, power(decay_log, steps), 0.0)
        weight = jnp.where((kind == 4) & (k == 0), 1.0, weight)
        weight = jnp.where((kind == 5) & (count - 1 == k), 1.0, weight)
        s_weight[k] = jnp.where(k < count, weight, 0.0)

    pl.semaphore_wait(barrier, planes + ranks - 2)
    send(forth_first, forth, 0)
    copies[1].wait()

    @pl.loop(0, length // LANES, unroll=2)
    def _(tile):
        at = lanes(tile * LANES)
        totals = [jnp.zeros((STATES, LANES), jnp.float32)] * 3
        for k in range(16):
            weight = s_weight[k]
            totals = [totals[c] + weight * v[c, k // 8, pl.ds(k % 8, 1), at] for c in range(3)]
        for c in range(3):
            s_out[c, :, at] = totals[c]

    over_ranks(lambda p, step: state_forth(my_row, p, step).start())
    s_in[my_row] = s_out[:, :, lanes(my_row * s_cols, s_cols)]
    for half in range(2):
        z_in[half, my_plane] = v[:, half, :, lanes(my_plane * z_cols, z_cols)]

    for copy in copies[2:]:
        copy.wait()
    line_high[...], line_low[...] = split(line[...])
    plane_high[...], plane_low[...] = split(plane[...])

    for c in range(3):
        turned = pltpu.roll(v[c].reshape(16, length), LANES // 2, 1)
        high, low = split(turned)
        rows = pl.ds(16 * c, 16)
        pad_high[rows, pl.ds(0, length)] = high
        pad_low[rows, pl.ds(0, length)] = low
        pad_high[rows, pl.ds(length, LANES)] = high[:, :LANES]
        pad_low[rows, pl.ds(length, LANES)] = low[:, :LANES]

    send(forth_first, forth, 1)
    pass_on(forth_first, forth_second, 0)

    group = 8

    def along_x(step):
        def windows(ref):
            return jnp.concatenate(
                [ref[:, lanes((step * group + i) * LANES, 2 * LANES)] for i in range(group)], axis=0
            )

        both = product((windows(pad_high), windows(pad_low)), (line_high[...], line_low[...]))
        for i in range(group):
            at = lanes((step * group + i) * LANES)
            wind = v[0, :, :, at].reshape(16, LANES)
            for c in range(3):
                rows = slice(48 * i + 16 * c, 48 * i + 16 * c + 16)
                part = both[rows, LANES:] - wind * both[rows, :LANES]
                out[c, :, :, at] = part.reshape(2, 8, LANES)

    def keep(half):
        own = z_back.at[:, half, :, lanes(my_plane * z_cols, z_cols)]
        return pltpu.make_async_copy(z_out.at[half, my_plane], own, local_sem.at[7 + half])

    def along_z(half):
        over_planes(lambda p, step: forth(half, p, my_plane, planes - step).wait_recv())
        live = iota((planes, 8, LANES), 1) + 8 * half < count
        for part in range(z_cols // LANES):
            cut = slice(part * LANES, (part + 1) * LANES)
            held = [z_in[half, :, c, :, cut].reshape(8 * planes, LANES) for c in range(3)]
            both = product((plane_high[...], plane_low[...]), split(jnp.concatenate(held, axis=1)))
            for c in range(3):
                at = slice(c * LANES, (c + 1) * LANES)
                term = both[8 * planes :, at] - held[2] * both[: 8 * planes, at]
                z_out[half, :, c, :, cut] = jnp.where(live, term.reshape(planes, 8, LANES), 0.0)
        send(back_first, back, half)
        keep(half).start()

    pl.loop(0, length // (LANES * group))(along_x)
    pass_on(forth_first, forth_second, 1)

    size = ranks * STATES
    col_rank, col_kind = iota((8, size), 1) // STATES, iota((8, size), 1) % STATES
    row_kind = iota((8, size), 0)
    row_log = jnp.where(row_kind % 2 == 0, FIRST["log"], SECOND["log"])
    col_start = col_count = jnp.zeros((8, size), jnp.int32)
    start = jnp.int32(0)
    for rank in range(ranks):
        col_start = col_start + jnp.where(rank < col_rank, counts[rank], 0)
        col_count = jnp.where(rank == col_rank, counts[rank], col_count)
        start = start + jnp.where(rank < my_row, counts[rank], 0)

    def rank_rows(rank, row_start):
        row_count = counts[rank]
        ahead = row_start - col_start - col_count
        ahead = jnp.where(ahead < 0, ahead + live_total, ahead)
        behind = col_start - row_start - row_count
        behind = jnp.where(behind < 0, behind + live_total, behind)
        same = power(row_log, jnp.where(row_kind < 2, ahead, behind))
        rows = jnp.where((row_kind == col_kind) & (row_kind < 4), same, 0.0)
        rows = jnp.where((row_kind == 4) & (col_kind == 5) & (ahead == 0), 1.0, rows)
        rows = jnp.where((row_kind == 5) & (col_kind == 4) & (behind == 0), 1.0, rows)
        matrix[pl.ds(pl.multiple_of(rank * STATES, STATES), STATES), :] = rows
        return row_start + row_count

    lax.fori_loop(0, ranks, rank_rows, jnp.int32(0), unroll=4)

    def over_y():
        over_ranks(lambda p, step: state_forth(p, my_row, ranks - step).wait_recv())
        held = [s_in[:, c].reshape(size, s_cols) for c in range(3)]
        both = product(split(matrix[...]), split(jnp.concatenate(held, axis=1)))
        for c in range(3):
            s_mid[:, c] = both[:, c * s_cols : (c + 1) * s_cols].reshape(ranks, STATES, s_cols)
        over_ranks(lambda p, step: state_back(my_row, p, step).start())
        s_back[:, :, lanes(my_row * s_cols, s_cols)] = s_mid[my_row]

    for half in range(2):
        slot = iota((8, LANES), 0) + 8 * half
        stretch = jnp.zeros((8, LANES), jnp.float32)
        bend = jnp.zeros((8, LANES), jnp.float32)
        for k in range(8 * half, 8 * half + 8):
            grid_row = jnp.minimum(start + k, live_total - 1)
            stretch = jnp.where(slot == k, metric[grid_row], stretch)
            bend = jnp.where(slot == k, curvature[grid_row], bend)
        live = slot < count
        tail = jnp.maximum(count - slot, 0)
        for term in range(16 + 6):
            if term < 16:
                away = jnp.abs(term - slot)
                one = FIRST["amp"] * power(FIRST["log"], away) + jnp.where(away == 1, FIRST["near"], 0.0)
                one = jnp.where(away == 0, 0.0, jnp.where(term > slot, one, -one))
                two = SECOND["amp"] * power(SECOND["log"], away) + jnp.where(away == 1, SECOND["near"], 0.0)
                two = jnp.where(away == 0, SECOND["centre"], two)
                used = live & (term < count)
            else:
                one = two = jnp.zeros((8, LANES), jnp.float32)
                used = live
                if term == 16:
                    one = -FIRST["amp"] * power(FIRST["log"], slot + 1)
                if term == 17:
                    two = SECOND["amp"] * power(SECOND["log"], slot + 1)
                if term == 18:
                    one = FIRST["amp"] * power(FIRST["log"], tail)
                if term == 19:
                    two = SECOND["amp"] * power(SECOND["log"], tail)
                if term == 20:
                    one = jnp.where(slot == 0, -FIRST["near"], 0.0)
                    two = jnp.where(slot == 0, SECOND["near"], 0.0)
                if term == 21:
                    one = jnp.where(tail == 1, FIRST["near"], 0.0)
                    two = jnp.where(tail == 1, SECOND["near"], 0.0)
            y_weight[term, half, 0] = jnp.where(used, stretch * one, 0.0)
            y_weight[term, half, 1] = jnp.where(
                used, viscosity * (stretch * stretch * two + bend * one), 0.0
            )

    along_z(0)
    along_z(1)
    pass_on(back_first, back_second, 0)
    over_y()
    pass_on(back_first, back_second, 1)
    for half in range(2):
        sent(forth_first, forth_second, forth, half)
    over_ranks(lambda p, step: state_forth(my_row, p, step).wait_send())
    over_ranks(lambda p, step: state_back(p, my_row, ranks - step).wait_recv())

    def along_y(tile):
        at = lanes(tile * LANES)
        sums = [[[jnp.zeros((8, LANES), jnp.float32)] * 2 for _ in range(2)] for _ in range(3)]
        for term in range(16 + 6):
            for c in range(3):
                if term < 16:
                    row = v[c, term // 8, pl.ds(term % 8, 1), at]
                else:
                    row = s_back[c, pl.ds(term - 16, 1), at]
                for half in range(2):
                    sums[c][half] = [sums[c][half][i] + y_weight[term, half, i] * row for i in range(2)]
        for half in range(2):
            wind = v[1, half, :, at]
            live = iota((8, LANES), 0) + 8 * half < count
            for c in range(3):
                term = out[c, half, :, at] + sums[c][half][1] - wind * sums[c][half][0]
                out[c, half, :, at] = jnp.where(live, term, 0.0)

    pl.loop(0, length // LANES)(along_y)
    leave = pltpu.make_async_copy(out, out_far, local_sem.at[6])
    leave.start()
    over_ranks(lambda p, step: state_back(my_row, p, step).wait_send())
    for half in range(2):
        sent(back_first, back_second, back, half)
    for half in range(2):
        over_planes(lambda p, step, half=half: back(half, p, my_plane, planes - step).wait_recv())
        keep(half).wait()
    leave.wait()


def add_kernel(left_far, right_far, out_far, left, right, load_sem, store_sem):
    def load(c, i):
        return pltpu.make_async_copy((left_far, right_far)[i].at[c], (left, right)[i].at[c], load_sem.at[c, i])

    def store(c):
        return pltpu.make_async_copy(left.at[c], out_far.at[c], store_sem.at[c])

    for c in range(3):
        for i in range(2):
            load(c, i).start()
    for c in range(3):
        for i in range(2):
            load(c, i).wait()
        left[c] = left[c] + right[c]
        store(c).start()
    for c in range(3):
        store(c).wait()


def local(ranks, planes, velocity, row_counts, y_metric, y_curvature):
    length = velocity.shape[3]
    live_total = y_metric.shape[0]
    z_cols, s_cols = length // planes, length // ranks
    far = pl.BlockSpec(memory_space=pltpu.HBM)
    whole = (3, 2, 8, length)
    line, plane = line_table().astype(np.float32), plane_table(planes).astype(np.float32)
    dma = pltpu.SemaphoreType.DMA
    f32, bf16 = jnp.float32, jnp.bfloat16
    parts = pl.pallas_call(
        functools.partial(kernel, ranks, planes, live_total, length),
        out_shape=[jax.ShapeDtypeStruct(whole, f32)] * 2,
        in_specs=[far] * 6,
        out_specs=[far] * 2,
        scratch_shapes=[
            pltpu.VMEM(whole, f32),
            pltpu.VMEM(whole, f32),
            pltpu.SMEM(row_counts.shape, jnp.int32),
            pltpu.SMEM(y_metric.shape, f32),
            pltpu.SMEM(y_curvature.shape, f32),
            pltpu.VMEM(line.shape, f32),
            pltpu.VMEM(plane.shape, f32),
            pltpu.VMEM(line.shape, bf16),
            pltpu.VMEM(line.shape, bf16),
            pltpu.VMEM(plane.shape, bf16),
            pltpu.VMEM(plane.shape, bf16),
            pltpu.VMEM((ranks * STATES, ranks * STATES), f32),
            pltpu.VMEM((48, length + LANES), bf16),
            pltpu.VMEM((48, length + LANES), bf16),
            pltpu.VMEM((2, planes, 3, 8, z_cols), f32),
            pltpu.VMEM((2, planes, 3, 8, z_cols), f32),
            pltpu.VMEM((2, 2, 2, 3, 8, z_cols), f32),
            pltpu.VMEM((3, STATES, length), f32),
            pltpu.VMEM((ranks, 3, STATES, s_cols), f32),
            pltpu.VMEM((ranks, 3, STATES, s_cols), f32),
            pltpu.VMEM((3, STATES, length), f32),
            pltpu.VMEM((16, STATES, LANES), f32),
            pltpu.VMEM((22, 2, 2, 8, LANES), f32),
            dma((9,)),
            dma((2, planes)),
            dma((2, planes)),
            dma((2, planes)),
            dma((2, planes)),
            dma((ranks,)),
            dma((ranks,)),
            dma((ranks,)),
            dma((ranks,)),
            dma((2, 3, 2, 2)),
        ],
        compiler_params=pltpu.CompilerParams(
            collective_id=0, has_side_effects=True, vmem_limit_bytes=63 * 1024 * 1024
        ),
        cost_estimate=pl.CostEstimate(flops=10**9, bytes_accessed=2 * 10**6, transcendentals=10**5),
    )(velocity.reshape(whole), row_counts, y_metric, y_curvature, jnp.asarray(line), jnp.asarray(plane))
    result = pl.pallas_call(
        add_kernel,
        out_shape=jax.ShapeDtypeStruct(whole, f32),
        in_specs=[far] * 2,
        out_specs=far,
        scratch_shapes=[pltpu.VMEM(whole, f32), pltpu.VMEM(whole, f32), dma((3, 2)), dma((3,))],
        compiler_params=pltpu.CompilerParams(vmem_limit_bytes=63 * 1024 * 1024),
        cost_estimate=pl.CostEstimate(flops=2 * 10**5, bytes_accessed=2 * 10**6, transcendentals=0),
    )(*parts)
    return result.reshape(velocity.shape)


def solution(mesh):
    return jax.shard_map(
        functools.partial(local, mesh.shape["row"], mesh.shape["span"]),
        mesh=mesh,
        in_specs=(P(None, "span", "row", None), P(), P(), P()),
        out_specs=P(None, "span", "row", None),
        check_vma=False,
    )
```
